512 devices in a mesh: col: 128 (over y, z, core), row: 4 (over x).
Axes of the slice: x: 4, y: 4, z: 16, core: 2. Of those that a mesh axis runs over, the one named last changes fastest.
Arguments:
- right_side: float32 [5, 256, 4096], P(None, 'col'), may hold values from -6 to 6
- diag_inverse: float32 [5, 256, 4096], P(None, 'col'), may hold values from -1 to 2
- panels: bfloat16 [4, 256, 64, 2048], P(None, 'col', None, 'row'), may hold values from -0.125 to 0.125
- tile_rows: int32 [4, 256, 32], P(None, 'col', 'row'), may hold values from 256 to 1279, as said below
Outputs:
- solution: float32 [5, 256, 4096], P(None, 'col')
The draws below stay inside these ranges and needn't reach their ends.
Inputs may be any that keep to these rules, and one draw needn't show every extreme that they name: tile_rows[t, q, s] is the global index of a block column of a level above t. Tiles of the same t whose block columns q share q // 2, whose s share s // 8, and whose block rows i share (i % 256) // 2, all name the same block row.
All inputs are finite; a program needn't handle non-finite values.
Results may differ from the reference program's by a relative error of at most 0.0059.
Values may be sent and summed in bfloat16 or wider, within the bound.
A program may use at most 64 MiB of HBM per device.

```python
import math
import jax
import jax.numpy as jnp
from jax import lax

BS = 64
R = 64
LEVELS = 5
BPL = 2
NNZ_DEV = 8
TLEV = 4
COLS_LEV = 256
NNZ = 32
OWNERS = 128


def draw_diag_inverse(key, part):
    key_noise = jax.random.fold_in(key, 31)
    key_scale = jax.random.fold_in(key, 32)
    noise = jnp.clip(jax.random.normal(key_noise, (LEVELS, COLS_LEV, BS, BS), jnp.float32), -4.0, 4.0)
    scales = jnp.exp(jax.random.uniform(key_scale, (LEVELS, COLS_LEV, BS), jnp.float32, math.log(0.5), math.log(1.5)))
    eye = jnp.eye(BS, dtype=jnp.float32)
    matrix = noise * (0.5 / math.sqrt(BS)) + eye * scales[..., None]
    return matrix.reshape(LEVELS, COLS_LEV, BS * BS).astype(jnp.float32)


def draw_tile_rows(key, part):
    key_owner = jax.random.fold_in(key, 41)
    key_level = jax.random.fold_in(key, 42)
    key_slot = jax.random.fold_in(key, 43)
    groups = NNZ // NNZ_DEV
    owner = jax.random.randint(key_owner, (TLEV, COLS_LEV, NNZ), 0, OWNERS)
    spread = jax.random.randint(key_level, (TLEV, OWNERS, groups, OWNERS), 0, 1 << 20)
    choose = jax.random.randint(key_slot, (TLEV, OWNERS, groups, OWNERS), 0, BPL)
    level_grid = jnp.broadcast_to(jnp.arange(TLEV, dtype=jnp.int32)[:, None, None], owner.shape)
    source_grid = jnp.broadcast_to((jnp.arange(COLS_LEV, dtype=jnp.int32) // BPL)[None, :, None], owner.shape)
    group_grid = jnp.broadcast_to((jnp.arange(NNZ, dtype=jnp.int32) // NNZ_DEV)[None, None, :], owner.shape)
    picked_level = spread[level_grid, source_grid, group_grid, owner] % (LEVELS - 1 - level_grid) + level_grid + 1
    picked_slot = choose[level_grid, source_grid, group_grid, owner]
    return (picked_level * COLS_LEV + owner * BPL + picked_slot).astype(jnp.int32)


def shard_levels(stream_key, dims, shards, low, top_value):
    def one(dim, blocks):
        steps = jax.random.uniform(jax.random.fold_in(jax.random.fold_in(stream_key, 6), dim), (blocks,), jnp.float32, low / len(shards), top_value / len(shards))
        return jnp.repeat(jnp.exp(steps), dims[dim] // blocks).reshape((-1,) + (1,) * (len(dims) - dim - 1))

    gain = one(*shards[0])
    for cut in shards[1:]:
        gain = gain * one(*cut)
    return gain


def normal_values(key, dims, deviation, bound, cuts=(), kind=jnp.bfloat16):
    entries = jax.random.normal(key, dims, jnp.float32) * deviation
    if len(cuts) > 0:
        entries = shard_levels(key, dims, cuts, -0.22, 0.18) * entries
    return jnp.clip(entries, min=-bound, max=bound).astype(kind)


def setup_inputs(seed: int = 0) -> dict:
    key_of = jax.random.split(jax.random.key(seed), 5)
    right_side = normal_values(key_of[0], (LEVELS, COLS_LEV, BS * R), 1.0, 6.0, ((1, 128),), jnp.float32)
    diag_inverse = draw_diag_inverse(jax.random.fold_in(key_of[4], 71), 0)
    panels = normal_values(key_of[2], (TLEV, COLS_LEV, BS, NNZ * BS), (BS * NNZ) ** -0.5, 0.125, ((1, 128), (3, 4)))
    tile_rows = draw_tile_rows(jax.random.fold_in(key_of[4], 71), 0)
    return {"right_side": right_side, "diag_inverse": diag_inverse, "panels": panels, "tile_rows": tile_rows}


def reference(right_side, diag_inverse, panels, tile_rows):
    highest = lax.Precision.HIGHEST
    blocks_all = LEVELS * COLS_LEV
    right_blocks = right_side.reshape(LEVELS, COLS_LEV, BS, R)
    inverse = diag_inverse.reshape(LEVELS, COLS_LEV, BS, BS)
    updates = jnp.zeros((blocks_all, BS, R), jnp.float32)
    solved = []
    for height in range(LEVELS):
        offset = height * COLS_LEV
        remain = right_blocks[height] - updates[offset:offset + COLS_LEV]
        forward = jnp.einsum("qab,qbr->qar", inverse[height], remain, precision=highest)
        solved.append(forward)
        if height < TLEV:
            rounded = forward.astype(jnp.bfloat16)

            def add_column(totals, inputs):
                column_panel, vectors, targets = inputs
                product = lax.dot_general(column_panel, vectors, (((0,), (0,)), ((), ())), preferred_element_type=jnp.float32)
                return totals.at[targets].add(product.reshape(NNZ, BS, R)), None

            updates, _ = lax.scan(add_column, updates, (panels[height], rounded, tile_rows[height]))
    solution = jnp.zeros((blocks_all, BS, R), jnp.float32)
    for height in range(LEVELS - 1, -1, -1):
        offset = height * COLS_LEV
        if height < TLEV:
            rounded = solution.astype(jnp.bfloat16)

            def back_column(inputs):
                column_panel, targets = inputs
                picked = rounded[targets].reshape(NNZ * BS, R)
                return jnp.dot(column_panel, picked, preferred_element_type=jnp.float32)

            backward = lax.map(back_column, (panels[height], tile_rows[height]))
            remain = solved[height] - backward
        else:
            remain = solved[height]
        result = jnp.einsum("qba,qbr->qar", inverse[height], remain, precision=highest)
        solution = solution.at[offset:offset + COLS_LEV].set(result)
    return solution.reshape(LEVELS, COLS_LEV, BS * R)
```

```python
import functools

import jax
import jax.numpy as jnp
from jax import lax
from jax.experimental import pallas as pl
from jax.experimental.pallas import tpu as pltpu
from jax.sharding import PartitionSpec as P

BS = 64
LEVELS = 5
BPL = 2
NNZ_DEV = 8
TLEV = 4
RW = 8
MESH = pl.DeviceIdType.MESH
F32 = jnp.float32
BF16 = jnp.bfloat16
HIGHEST = lax.Precision.HIGHEST
NT_DIMS = (((1,), (1,)), ((), ()))
NN_DIMS = (((1,), (0,)), ((), ()))


def sizes(owners, rows):
    nz = 16 if owners % 32 == 0 else owners // 4
    ny = owners // 2 // nz
    return ny, nz


def kernel(
    owners,
    rows,
    bt,
    dd,
    tr,
    pan,
    out,
    trg,
    bu,
    ddc,
    pg,
    tbl,
    keepv,
    tbs,
    keeps,
    pd,
    cs,
    acc,
    sb,
    own,
    ry,
    sz,
    rz,
    ys,
    xu,
    xs,
    xg,
    fx,
    osc,
    cell_sem,
    pan_sem,
    loc_sem,
    tab_sem,
    y_send,
    y_recv,
    z_send,
    z_recv,
    f_send,
    f_recv,
):
    ny, nz = sizes(owners, rows)
    units = owners // 2
    cols = owners * BPL
    cells = 2 * rows
    tiles = cells * BPL * NNZ_DEV
    chunks = (TLEV * cols + 127) // 128
    col = lax.axis_index("col")
    x = lax.axis_index("row")
    c = col % 2
    z = (col // 2) % nz
    y = col // 2 // nz
    me = x * 2 + c
    unit = y * nz + z

    def at(x_to, y_to, z_to, c_to):
        return {"row": x_to, "col": (y_to * nz + z_to) * 2 + c_to}

    def cell_peer(j):
        other = (me + j) % cells
        return other, at(other // 2, y, z, other % 2)

    def y_peer(j):
        y_to = (y + j) % ny
        return y_to, at(x, y_to, z, c)

    def z_peer(j):
        half = (j + 1) // 2
        step = nz // 2 + jnp.where(j % 2 == 0, half, -half)
        z_to = (z + step) % nz
        return z_to, at(x, y, z_to, c)

    def send(src, dst, send_sem, recv_sem, device):
        pltpu.make_async_remote_copy(
            src_ref=src,
            dst_ref=dst,
            send_sem=send_sem,
            recv_sem=recv_sem,
            device_id=device,
            device_id_type=MESH,
        ).start()

    def settle(ref, sem):
        pltpu.make_async_copy(ref, ref, sem).wait()

    low = lax.broadcasted_iota(jnp.int32, (RW, 128), 1) < BS

    barrier = pltpu.get_barrier_semaphore()

    def greet(device):
        pl.semaphore_signal(barrier, inc=1, device_id=device, device_id_type=MESH)

    for j in range(1, cells):
        greet(cell_peer(j)[1])
    for j in range(1, ny):
        greet(y_peer(j)[1])

    @pl.loop(0, nz - 1)
    def _(j):
        greet(z_peer(j)[1])

    pl.semaphore_wait(barrier, cells - 1 + ny - 1 + nz - 1)

    for j in range(1, cells):
        device = cell_peer(j)[1]
        send(tr, trg.at[me], cell_sem.at[0], cell_sem.at[1], device)
    core_peer = at(x, y, z, 1 - c)
    send(bt.at[x * 2 + 1 - c], bu.at[c], cell_sem.at[2], cell_sem.at[3], core_peer)
    send(dd, ddc.at[c], cell_sem.at[4], cell_sem.at[5], core_peer)
    for t in range(TLEV):
        pltpu.make_async_copy(pan.at[t], pg.at[t, me], loc_sem.at[t]).start()
        for j in range(1, cells):
            device = cell_peer(j)[1]
            send(pan.at[t], pg.at[t, me], pan_sem.at[0, t], pan_sem.at[1, t], device)
    trg[me] = tr[...]
    bu[c] = bt[me]
    ddc[c] = dd[...]

    settle(trg.at[pl.ds(0, cells - 1)], cell_sem.at[1])
    targets = trg[0]
    for j in range(1, cells):
        targets = targets + trg[j]
    square = (128, 128)
    above = lax.broadcasted_iota(jnp.int32, square, 0)
    lane = lax.broadcasted_iota(jnp.int32, square, 1)
    for t in range(TLEV):
        mine = jnp.broadcast_to(targets[t : t + 1, :], square)
        other = mine.T
        before = (other < mine) | ((other == mine) & (above < lane))
        rank = jnp.sum(before.astype(jnp.int32), axis=0, keepdims=True)
        placed = jnp.broadcast_to(rank, square).T == lane
        order = jnp.sum(jnp.where(placed, above, 0), axis=0, keepdims=True)
        ordered = jnp.sum(jnp.where(placed, other, 0), axis=0, keepdims=True)
        ordered8 = jnp.broadcast_to(ordered, (8, 128))
        first = lax.broadcasted_iota(jnp.int32, (8, 128), 1) == 0
        same = (ordered8 == pltpu.roll(ordered8, 1, 1)) & jnp.logical_not(first)
        keepv[t : t + 1, :] = same.astype(F32)[0:1]
        tbl[t : t + 1, :] = order
        tbl[TLEV + t : TLEV + t + 1, :] = jnp.clip(mine[0:1] - cols, 0, TLEV * cols - 1)
        for chunk in range(t * cols // 128, chunks):
            slot = lane + (cols + chunk * 128)
            upto = jnp.sum((other <= slot).astype(jnp.int32), axis=0, keepdims=True)
            equal = jnp.sum((other == slot).astype(jnp.int32), axis=0, keepdims=True)
            row = 2 * TLEV + t * chunks + chunk
            tbl[row : row + 1, :] = jnp.where(equal > 0, upto - 1, 128)
    pltpu.make_async_copy(tbl, tbs, tab_sem.at[0]).start()
    pltpu.make_async_copy(keepv, keeps, tab_sem.at[1]).start()
    pltpu.make_async_copy(tbl, tbs, tab_sem.at[0]).wait()
    pltpu.make_async_copy(keepv, keeps, tab_sem.at[1]).wait()
    cs[128] = jnp.zeros((RW, 128), F32)
    settle(bu.at[0], cell_sem.at[3])
    settle(ddc.at[0], cell_sem.at[5])

    def last_sum(t, level, s):
        number = (level - 1) * cols + s
        place = tbs[2 * TLEV + t * chunks + number // 128, number % 128]
        return cs[place]

    def pair(t, level, u, h):
        s = u * 4 + 2 * h
        return jnp.where(low, last_sum(t, level, s), last_sum(t, level, s + 1))

    update = None
    for t in range(LEVELS):
        solved = []
        for core in range(2):
            remain = bu[core, t]
            if t > 0:
                remain = remain - update[core]
            value = lax.dot_general(
                remain, ddc[core, t], NT_DIMS, precision=HIGHEST, preferred_element_type=F32
            )
            ys[t, core] = value
            solved.append(value)
        if t == TLEV:
            break
        nothing = jnp.zeros((RW, 128), F32)
        left = jnp.concatenate(
            [
                jnp.where(low, solved[0], 0.0),
                jnp.where(low, 0.0, solved[0]),
                nothing,
                nothing,
            ],
            axis=0,
        )
        right = jnp.concatenate(
            [
                nothing,
                nothing,
                jnp.where(low, solved[1], 0.0),
                jnp.where(low, 0.0, solved[1]),
            ],
            axis=0,
        )
        vectors = jnp.concatenate([left, right], axis=1).astype(BF16)
        settle(pg.at[t, 0], loc_sem.at[t])
        settle(pg.at[t, pl.ds(0, cells - 1)], pan_sem.at[1, t])
        for group in range(rows):
            panel = jnp.concatenate([pg[t, 2 * group], pg[t, 2 * group + 1]], axis=0)
            product = lax.dot_general(vectors, panel, NN_DIMS, preferred_element_type=F32)
            for b in range(4):
                for p in range(4):
                    value = product[b * RW : (b + 1) * RW, p * 128 : (p + 1) * 128]
                    turned = pltpu.roll(value, BS, 1)
                    tile = group * 32 + b * 8 + p * 2
                    pd[tile] = jnp.where(low, value, turned)
                    pd[tile + 1] = jnp.where(low, turned, value)

        def scan(i, total, t=t):
            for k in range(8):
                place = i * 8 + k
                total = total * keeps[t, place] + pd[tbs[t, place]]
                cs[place] = total
            return total

        lax.fori_loop(0, tiles // 8, scan, jnp.zeros((RW, 128), F32))

        level = t + 1
        for j in list(range(1, ny)) + [0]:
            y_to, device = y_peer(j)

            @pl.loop(0, nz)
            def _(i, t=t, level=level, j=j, y_to=y_to):
                u = y_to * nz + i
                halves = []
                for h in range(2):
                    value = pair(t, level, u, h)
                    if t > 0:
                        value = value + acc[level - 2, u * 2 + h]
                    halves.append(value)
                if j == 0:
                    own[i, 0] = halves[0]
                    own[i, 1] = halves[1]
                else:
                    sb[t, u] = jnp.concatenate(halves, axis=0).astype(BF16)

            if j > 0:
                send(
                    sb.at[t, pl.ds(y_to * nz, nz)],
                    ry.at[t, j - 1],
                    y_send.at[t],
                    y_recv.at[t],
                    device,
                )
        for level in range(t + 2, LEVELS):

            @pl.loop(0, units)
            def _(u, t=t, level=level):
                for h in range(2):
                    value = pair(t, level, u, h)
                    if t > 0:
                        value = value + acc[level - 2, u * 2 + h]
                    acc[level - 2, u * 2 + h] = value

        settle(ry.at[t], y_recv.at[t])

        def partial(i, t=t):
            halves = []
            for h in range(2):
                value = own[i, h]
                for j in range(ny - 1):
                    value = value + ry[t, j, i].astype(F32)[h * RW : (h + 1) * RW]
                halves.append(value)
            return halves

        @pl.loop(0, nz - 1)
        def _(j, t=t):
            z_to, device = z_peer(j)
            sz[t, j] = jnp.concatenate(partial(z_to), axis=0).astype(BF16)
            send(sz.at[t, j], rz.at[t, j], z_send.at[t], z_recv.at[t], device)

        update = partial(z)
        settle(rz.at[t], z_recv.at[t])
        for j in range(nz - 1):
            arrived = rz[t, j].astype(F32)
            update = [update[0] + arrived[:RW], update[1] + arrived[RW:]]

    for t in range(LEVELS - 1, -1, -1):
        if t < TLEV:
            weighted = jnp.zeros((4 * RW, 4 * BS), F32)
            for group in range(rows):
                for b in range(4):
                    for p in range(4):
                        tile = group * 32 + b * 8 + p * 2
                        value = jnp.where(
                            low, xs[tbs[TLEV + t, tile]], xs[tbs[TLEV + t, tile + 1]]
                        )
                        xg[group, b * RW : (b + 1) * RW, p * 128 : (p + 1) * 128] = value
                panel = jnp.concatenate([pg[t, 2 * group], pg[t, 2 * group + 1]], axis=0)
                weighted = weighted + lax.dot_general(
                    xg[group].astype(BF16), panel, NT_DIMS, preferred_element_type=F32
                )
        results = []
        for core in range(2):
            remain = ys[t, core]
            if t < TLEV:
                remain = remain - jnp.where(
                    low,
                    weighted[core * 16 : core * 16 + 8, core * 128 : core * 128 + 128],
                    weighted[core * 16 + 8 : core * 16 + 16, core * 128 : core * 128 + 128],
                )
            value = lax.dot_general(
                remain, ddc[core, t], NN_DIMS, precision=HIGHEST, preferred_element_type=F32
            )
            fx[t, core] = value
            results.append(value)
        if t > 0:
            xu[t - 1, unit] = jnp.concatenate(results, axis=0).astype(BF16)

            @pl.loop(0, nz - 1)
            def _(j, t=t):
                z_to, device = z_peer(j)
                here = xu.at[t - 1, unit]
                send(here, here, z_send.at[TLEV + t - 1], z_recv.at[TLEV + t - 1], device)

        osc[me, t] = fx[t, c]
        for j in range(1, cells):
            other, device = cell_peer(j)
            send(fx.at[t, other % 2], osc.at[me, t], f_send, f_recv, device)

        if t > 0:

            def expand(u, t=t):
                value = xu[t - 1, u].astype(F32)
                for h in range(2):
                    half = value[h * RW : (h + 1) * RW]
                    turned = pltpu.roll(half, BS, 1)
                    slot = (t - 1) * cols + u * 4 + h * 2
                    xs[slot] = jnp.where(low, half, turned)
                    xs[slot + 1] = jnp.where(low, turned, half)

            settle(xu.at[t - 1, pl.ds(0, nz - 1)], z_recv.at[TLEV + t - 1])
            for j in range(1, ny):
                y_to, device = y_peer(j)
                here = xu.at[t - 1, pl.ds(y * nz, nz)]
                send(here, here, y_send.at[TLEV + t - 1], y_recv.at[TLEV + t - 1], device)

            @pl.loop(0, nz)
            def _(i):
                expand(y * nz + i)

            settle(xu.at[t - 1, pl.ds(0, (ny - 1) * nz)], y_recv.at[TLEV + t - 1])

            @pl.loop(0, (ny - 1) * nz)
            def _(i):
                expand((y * nz + nz + i) % units)

    settle(trg.at[pl.ds(0, cells - 1)], cell_sem.at[0])
    settle(bu.at[0], cell_sem.at[2])
    settle(ddc.at[0], cell_sem.at[4])
    for t in range(TLEV):
        settle(pg.at[t, pl.ds(0, cells - 1)], pan_sem.at[0, t])
        settle(ry.at[t], y_send.at[t])
        settle(rz.at[t], z_send.at[t])
        settle(xu.at[t, pl.ds(0, (ny - 1) * nz)], y_send.at[TLEV + t])
        settle(xu.at[t, pl.ds(0, nz - 1)], z_send.at[TLEV + t])
    settle(osc.at[pl.ds(0, cells - 1)], f_send)
    settle(osc.at[pl.ds(0, cells - 1)], f_recv)
    out[...] = osc[...]


def local(right_side, diag_inverse, panels, tile_rows):
    owners = lax.axis_size("col")
    rows = lax.axis_size("row")
    ny, nz = sizes(owners, rows)
    units = owners // 2
    cols = owners * BPL
    cells = 2 * rows
    chunks = (TLEV * cols + 127) // 128
    table_rows = 2 * TLEV + TLEV * chunks
    me = lax.axis_index("row") * 2 + lax.axis_index("col") % 2
    bt = right_side.reshape(LEVELS, BPL, BS, cells, RW).transpose(3, 0, 4, 1, 2)
    bt = bt.reshape(cells, LEVELS, RW, BPL * BS)
    inverse = diag_inverse.reshape(LEVELS, BPL, BS, BS)
    eye = jnp.eye(BPL, dtype=F32)[None, :, None, :, None]
    dd = jnp.where(eye > 0, inverse[:, :, :, None, :], 0.0).reshape(LEVELS, BPL * BS, BPL * BS)
    pan = panels.reshape(TLEV, BPL * BS, NNZ_DEV * BS)
    per = BPL * NNZ_DEV
    spread = jnp.tile(tile_rows.reshape(TLEV, per), (2, 128 // per))
    lane = lax.broadcasted_iota(jnp.int32, (8, 128), 1)
    tr = jnp.where(lane // per == me, spread, 0)
    if cells * per < 128:
        tr = jnp.where(lane >= cells * per, 1 << 20, tr)
    vmem = pl.BlockSpec(memory_space=pltpu.VMEM)
    result = pl.pallas_call(
        functools.partial(kernel, owners, rows),
        out_shape=jax.ShapeDtypeStruct((cells, LEVELS, RW, BPL * BS), F32),
        in_specs=[vmem, vmem, vmem, pl.BlockSpec(memory_space=pl.ANY)],
        out_specs=vmem,
        scratch_shapes=[
            pltpu.VMEM((cells, 8, 128), jnp.int32),
            pltpu.VMEM((2, LEVELS, RW, 128), F32),
            pltpu.VMEM((2, LEVELS, 128, 128), F32),
            pltpu.VMEM((TLEV, cells, BPL * BS, NNZ_DEV * BS), BF16),
            pltpu.VMEM((table_rows, 128), jnp.int32),
            pltpu.VMEM((8, 128), F32),
            pltpu.SMEM((table_rows, 128), jnp.int32),
            pltpu.SMEM((8, 128), F32),
            pltpu.VMEM((128, RW, 128), F32),
            pltpu.VMEM((129, RW, 128), F32),
            pltpu.VMEM((TLEV - 1, units * 2, RW, 128), F32),
            pltpu.VMEM((TLEV, units, 2 * RW, 128), BF16),
            pltpu.VMEM((nz, 2, RW, 128), F32),
            pltpu.VMEM((TLEV, ny - 1, nz, 2 * RW, 128), BF16),
            pltpu.VMEM((TLEV, nz - 1, 2 * RW, 128), BF16),
            pltpu.VMEM((TLEV, nz - 1, 2 * RW, 128), BF16),
            pltpu.VMEM((LEVELS, 2, RW, 128), F32),
            pltpu.VMEM((TLEV, units, 2 * RW, 128), BF16),
            pltpu.VMEM((TLEV * cols, RW, 128), F32),
            pltpu.VMEM((rows, 4 * RW, NNZ_DEV * BS), F32),
            pltpu.VMEM((LEVELS, 2, RW, 128), F32),
            pltpu.VMEM((cells, LEVELS, RW, 128), F32),
            pltpu.SemaphoreType.DMA((6,)),
            pltpu.SemaphoreType.DMA((2, TLEV)),
            pltpu.SemaphoreType.DMA((TLEV,)),
            pltpu.SemaphoreType.DMA((2,)),
            pltpu.SemaphoreType.DMA((2 * TLEV,)),
            pltpu.SemaphoreType.DMA((2 * TLEV,)),
            pltpu.SemaphoreType.DMA((2 * TLEV,)),
            pltpu.SemaphoreType.DMA((2 * TLEV,)),
            pltpu.SemaphoreType.DMA,
            pltpu.SemaphoreType.DMA,
        ],
        compiler_params=pltpu.CompilerParams(
            collective_id=0, has_side_effects=True, vmem_limit_bytes=40 * 1024 * 1024
        ),
    )(bt, dd, tr, pan)
    result = result.reshape(cells, LEVELS, RW, BPL, BS).transpose(1, 3, 4, 0, 2)
    return result.reshape(LEVELS, BPL, BS * cells * RW)


def solution(mesh):
    in_specs = (
        P(None, "col", None),
        P(None, "col", None),
        P(None, "col", None, "row"),
        P(None, "col", "row"),
    )
    out_specs = P(None, "col", None)
    return jax.shard_map(local, mesh=mesh, in_specs=in_specs, out_specs=out_specs, check_vma=False)
```

```python
import functools

import jax
import jax.numpy as jnp
from jax import lax
from jax.experimental import pallas as pl
from jax.experimental.pallas import tpu as pltpu
from jax.sharding import PartitionSpec as P

BS = 64
LEVELS = 5
BPL = 2
NNZ_DEV = 8
TLEV = 4
RW = 8
MESH = pl.DeviceIdType.MESH
F32 = jnp.float32
BF16 = jnp.bfloat16
NT_DIMS = (((1,), (1,)), ((), ()))
NN_DIMS = (((1,), (0,)), ((), ()))


def sizes(owners):
    nz = 16 if owners % 32 == 0 else owners // 4
    return owners // 2 // nz, nz


def split(value):
    high = value.astype(BF16)
    return high, (value - high.astype(F32)).astype(BF16)


def product(value, pair, dims):
    rows = value.shape[0]
    high, rest = split(value)
    both = jnp.concatenate([high.astype(F32), rest.astype(F32)], axis=0).astype(BF16)
    first = lax.dot_general(both, pair[0], dims, preferred_element_type=F32)
    second = lax.dot_general(high, pair[1], dims, preferred_element_type=F32)
    return first[:rows] + (first[rows:] + second)


def kernel(
    owners,
    rows,
    rs,
    di,
    tr,
    pan,
    out,
    trg,
    flip,
    bt,
    bu,
    ddc,
    pg,
    p0s,
    p0r,
    tbl,
    keepv,
    tbs,
    keeps,
    pd,
    cs,
    acc,
    sb,
    own,
    ry,
    sz,
    rz,
    ys,
    xu,
    xs,
    fx,
    osc,
    cell_sem,
    pan_sem,
    loc_sem,
    tab_sem,
    y_send,
    y_recv,
    z_send,
    z_recv,
    f_send,
    f_recv,
):
    ny, nz = sizes(owners)
    units = owners // 2
    cols = owners * BPL
    cells = 2 * rows
    per = BPL * NNZ_DEV
    tiles = cells * per
    chunks = (TLEV * cols + 127) // 128
    nfar = max(1, nz // 2 - 1)
    groups = ((0, nfar), (nfar, nz))
    col = lax.axis_index("col")
    x = lax.axis_index("row")
    c = col & 1
    z = (col // 2) & (nz - 1)
    y = col // (2 * nz)
    me = x * 2 + c

    def at(x_to, y_to, z_to, c_to):
        return {"row": x_to, "col": (y_to * nz + z_to) * 2 + c_to}

    def cell_peer(j):
        other = (me + j) & (cells - 1)
        return other, at(other // 2, y, z, other & 1)

    def y_peer(j):
        return at(x, (y + j) & (ny - 1), z, c)

    def step(p):
        half = (p + 1) // 2
        return nz // 2 + (half if p % 2 == 0 else -half)

    def facing(p):
        return p if step(p) in (0, nz // 2) else p + 1 if p % 2 == 1 else p - 1

    def z_peer(p):
        return at(x, y, (z + step(p)) & (nz - 1), c)

    def unit_of(j, p):
        return ((y + j) & (ny - 1)) * nz + ((z + step(p)) & (nz - 1))

    def send(src, dst, send_sem, recv_sem, device):
        pltpu.make_async_remote_copy(
            src_ref=src,
            dst_ref=dst,
            send_sem=send_sem,
            recv_sem=recv_sem,
            device_id=device,
            device_id_type=MESH,
        ).start()

    def settle(ref, sem):
        pltpu.make_async_copy(ref, ref, sem).wait()

    def low_of(count):
        return lax.broadcasted_iota(jnp.int32, (count, 128), 1) < BS

    low = low_of(RW)
    low32 = low_of(32)

    for t in range(TLEV):
        pltpu.make_async_copy(pan.at[t], pg.at[t, me], loc_sem.at[t]).start()

    barrier = pltpu.get_barrier_semaphore()

    def greet(device):
        pl.semaphore_signal(barrier, inc=1, device_id=device, device_id_type=MESH)

    for p in range(nz - 1):
        greet(z_peer(p))
    for j in range(1, ny):
        greet(y_peer(j))
    for j in range(1, cells):
        greet(cell_peer(j)[1])

    for t in range(LEVELS):
        for k in range(BPL):
            value = rs[t, pl.ds(k, 32, 2), :]
            flip[t, pl.ds(k * BS, 32, 2), :] = value
            flip[t, pl.ds(k * BS + 1, 32, 2), :] = pltpu.roll(value, BS, 1)
            value = di[t, pl.ds(k, 32, 2), :]
            turned = pltpu.roll(value, BS, 1)
            keep = low32 if k == 0 else jnp.logical_not(low32)
            for par in range(2):
                half = value if par == k else turned
                flip[LEVELS + t, pl.ds(k * BS + par, 32, 2), :] = jnp.where(keep, half, 0.0)
    cells_r = cells * RW
    for t in range(LEVELS):
        turned = flip[t].T
        for q in range(cells):
            bt[t, q] = turned[q * RW : (q + 1) * RW]
        high, rest = split(flip[LEVELS + t])
        ddc[c, t, 0] = high
        ddc[c, t, 1] = rest
    trg[me] = tr[...]
    for t in range(LEVELS):
        bu[c, t] = bt[t, me]

    right = bt[0].reshape(cells_r, 128)
    solved = product(right, (ddc[c, 0, 0], ddc[c, 0, 1]), NT_DIMS)
    pieces = []
    for q in range(cells):
        value = solved[q * RW : (q + 1) * RW]
        pieces += [jnp.where(low, value, 0.0), jnp.where(low, 0.0, value)]
    pltpu.make_async_copy(pan.at[0], pg.at[0, me], loc_sem.at[0]).wait()
    value = lax.dot_general(
        jnp.concatenate(pieces, axis=0).astype(BF16),
        pg[0, me],
        NN_DIMS,
        preferred_element_type=F32,
    ).astype(BF16)
    for q in range(cells):
        p0s[q] = value[q * 2 * RW : (q + 1) * 2 * RW]

    pl.semaphore_wait(barrier, cells - 1 + ny - 1 + nz - 1)

    for j in range(1, cells):
        other, device = cell_peer(j)
        send(tr, trg.at[me], cell_sem.at[0], cell_sem.at[1], device)
    for j in range(1, cells):
        other, device = cell_peer(j)
        send(p0s.at[other], p0r.at[me], cell_sem.at[6], cell_sem.at[7], device)
    core_peer = at(x, y, z, 1 - c)
    send(bt.at[:, me + 1 - 2 * c], bu.at[c], cell_sem.at[2], cell_sem.at[3], core_peer)
    send(ddc.at[c], ddc.at[c], cell_sem.at[4], cell_sem.at[5], core_peer)

    def send_panels(t):
        for j in range(1, cells):
            device = cell_peer(j)[1]
            send(pan.at[t], pg.at[t, me], pan_sem.at[0, t], pan_sem.at[1, t], device)

    send_panels(1)
    p0r[me] = p0s[me]

    settle(trg.at[pl.ds(0, cells - 1)], cell_sem.at[1])
    targets = trg[0]
    for j in range(1, cells):
        targets = targets + trg[j]
    square = (128, 128)
    above = lax.broadcasted_iota(jnp.int32, square, 0)
    lane = lax.broadcasted_iota(jnp.int32, square, 1)
    for t in range(TLEV):
        mine = jnp.broadcast_to(targets[t : t + 1, :], square)
        other = mine.T
        before = (other < mine) | ((other == mine) & (above < lane))
        rank = jnp.sum(before.astype(jnp.int32), axis=0, keepdims=True)
        placed = jnp.broadcast_to(rank, square).T == lane
        order = jnp.sum(jnp.where(placed, above, 0), axis=0, keepdims=True)
        ordered = jnp.sum(jnp.where(placed, other, 0), axis=0, keepdims=True)
        ordered8 = jnp.broadcast_to(ordered, (8, 128))
        first = lax.broadcasted_iota(jnp.int32, (8, 128), 1) == 0
        same = (ordered8 == pltpu.roll(ordered8, 1, 1)) & jnp.logical_not(first)
        keepv[t : t + 1, :] = same.astype(F32)[0:1]
        tbl[t : t + 1, :] = order
        source = jnp.clip(mine[0:1] - cols, 0, TLEV * cols - 1)
        tbl[TLEV + t : TLEV + t + 1, :] = source
        for chunk in range(t * cols // 128, chunks):
            slot = lane + (cols + chunk * 128)
            upto = jnp.sum((other <= slot).astype(jnp.int32), axis=0, keepdims=True)
            equal = jnp.sum((other == slot).astype(jnp.int32), axis=0, keepdims=True)
            row = 2 * TLEV + t * chunks + chunk
            tbl[row : row + 1, :] = jnp.where(equal > 0, upto - 1, 128)
    pltpu.make_async_copy(tbl, tbs, tab_sem.at[0]).start()
    pltpu.make_async_copy(keepv, keeps, tab_sem.at[1]).start()
    pltpu.make_async_copy(tbl, tbs, tab_sem.at[0]).wait()
    pltpu.make_async_copy(keepv, keeps, tab_sem.at[1]).wait()
    cs[128] = jnp.zeros((RW, 128), F32)

    def halves_of(t, level, u):
        number = (level - 1) * cols + u * 4
        row = 2 * TLEV + t * chunks + lax.shift_right_logical(number, 7)
        place = number & 127
        parts = [cs[tbs[row, place + k]] for k in range(4)]
        halves = [jnp.where(low, parts[0], parts[1]), jnp.where(low, parts[2], parts[3])]
        if t > 0:
            halves = [halves[h] + acc[level - 2, u * 2 + h] for h in range(2)]
        return halves

    def tile_pair(tile, value):
        turned = pltpu.roll(value, BS, 1)
        pd[tile] = jnp.where(low, value, turned)
        pd[tile + 1] = jnp.where(low, turned, value)

    def solve(t, core, remain, dims):
        return product(remain, (ddc[core, t, 0], ddc[core, t, 1]), dims)

    def forward(t, update):
        solved = []
        for core in range(2):
            remain = bu[core, t]
            if update is not None:
                remain = remain - update[core]
            value = solve(t, core, remain, NT_DIMS)
            ys[t, core] = value
            solved.append(value)
        return solved

    update = None
    for t in range(TLEV):
        if t == 0:
            settle(p0r.at[pl.ds(0, cells - 1)], cell_sem.at[7])
            for q in range(cells):
                value = p0r[q].astype(F32)
                for k in range(2):
                    for p in range(4):
                        part = value[k * RW : (k + 1) * RW, p * 128 : (p + 1) * 128]
                        tile_pair(q * per + k * NNZ_DEV + p * 2, part)
        else:
            solved = forward(t, update)
            nothing = jnp.zeros((RW, 128), F32)
            pieces = []
            for core in range(2):
                for k in range(2):
                    kept = jnp.where(low, solved[core], 0.0)
                    if k == 1:
                        kept = jnp.where(low, 0.0, solved[core])
                    side = [kept, nothing] if core == 0 else [nothing, kept]
                    pieces.append(jnp.concatenate(side, axis=1))
            vectors = jnp.concatenate(pieces, axis=0).astype(BF16)
            settle(pg.at[t, 0], loc_sem.at[t])
            settle(pg.at[t, pl.ds(0, cells - 1)], pan_sem.at[1, t])
            for group in range(rows):
                panel = pg[t, pl.ds(2 * group, 2)].reshape(4 * BS, NNZ_DEV * BS)
                value = lax.dot_general(vectors, panel, NN_DIMS, preferred_element_type=F32)
                for b in range(4):
                    for p in range(4):
                        part = value[b * RW : (b + 1) * RW, p * 128 : (p + 1) * 128]
                        tile_pair(group * 32 + b * 8 + p * 2, part)

        def scan(i, total, t=t):
            for k in range(16):
                place = i * 16 + k
                total = total * keeps[t, place] + pd[tbs[t, place]]
                cs[place] = total
            return total

        lax.fori_loop(0, tiles // 16, scan, jnp.zeros((RW, 128), F32))

        for g, (begin, end) in enumerate(groups):

            @pl.loop(0, ny - 1)
            def _(i, t=t, g=g, begin=begin, end=end):
                j = jnp.where(i == 0, ny // 2, jnp.where(i < ny // 2 + (ny == 2), i, i + 1))
                for p in range(begin, end):
                    halves = halves_of(t, t + 1, unit_of(j, p))
                    sb[t, j, p] = jnp.concatenate(halves, axis=0).astype(BF16)
                there = pl.ds(begin, end - begin)
                send(
                    sb.at[t, j, there],
                    ry.at[t, j - 1, there],
                    y_send.at[2 * t + g],
                    y_recv.at[2 * t + g],
                    y_peer(j),
                )

        for p in range(nz):
            halves = halves_of(t, t + 1, unit_of(0, p))
            own[p, 0] = halves[0]
            own[p, 1] = halves[1]
        if t + 2 < TLEV:
            send_panels(t + 2)
        for level in range(t + 2, LEVELS):

            @pl.loop(0, units // 4)
            def _(i, t=t, level=level):
                for k in range(4):
                    u = i * 4 + k
                    halves = halves_of(t, level, u)
                    acc[level - 2, u * 2] = halves[0]
                    acc[level - 2, u * 2 + 1] = halves[1]

        if t == 0:
            settle(bu.at[0], cell_sem.at[3])
            settle(ddc.at[0], cell_sem.at[5])
            forward(0, None)

        def partial(p, t=t):
            halves = []
            for h in range(2):
                value = own[p, h]
                for j in range(ny - 1):
                    value = value + ry[t, j, p].astype(F32)[h * RW : (h + 1) * RW]
                halves.append(value)
            return halves

        for g, (begin, end) in enumerate(groups):
            settle(ry.at[t, :, pl.ds(begin, end - begin)], y_recv.at[2 * t + g])
            for p in range(begin, min(end, nz - 1)):
                sz[t, p] = jnp.concatenate(partial(p), axis=0).astype(BF16)
                send(sz.at[t, p], rz.at[t, p], z_send.at[2 * t], z_recv.at[2 * t], z_peer(p))
        update = partial(nz - 1)
        settle(rz.at[t], z_recv.at[2 * t])
        for p in range(nz - 1):
            arrived = rz[t, p].astype(F32)
            update = [update[0] + arrived[:RW], update[1] + arrived[RW:]]

    send_panels(0)
    forward(TLEV, update)

    def finish(t):
        settle(osc.at[t, pl.ds(0, cells - 1)], f_recv.at[t])
        value = osc[t].reshape(cells_r, 128)
        if cells_r < 128:
            value = jnp.concatenate([value] * (128 // cells_r), axis=0)
        flip[t] = value.T
        for k in range(BPL):
            even = flip[t, pl.ds(k * BS, 32, 2), :]
            odd = flip[t, pl.ds(k * BS + 1, 32, 2), :]
            out[t, pl.ds(k, 32, 2), :] = jnp.where(low32, even, odd)

    for t in range(LEVELS - 1, -1, -1):
        if t < TLEV:
            if t == 0:
                settle(pg.at[0, pl.ds(0, cells - 1)], pan_sem.at[1, 0])
            weighted = None
            for group in range(rows):
                lines = []
                for b in range(4):
                    line = []
                    for p in range(4):
                        tile = group * 32 + b * 8 + p * 2
                        first = xs[tbs[TLEV + t, tile]]
                        second = xs[tbs[TLEV + t, tile + 1]]
                        line.append(jnp.where(low, first, second))
                    lines.append(jnp.concatenate(line, axis=1))
                picked = jnp.concatenate(lines, axis=0).astype(BF16)
                panel = pg[t, pl.ds(2 * group, 2)].reshape(4 * BS, NNZ_DEV * BS)
                value = lax.dot_general(picked, panel, NT_DIMS, preferred_element_type=F32)
                weighted = value if weighted is None else weighted + value
        results = []
        for core in range(2):
            remain = ys[t, core]
            if t < TLEV:
                lanes = slice(core * 128, core * 128 + 128)
                remain = remain - jnp.where(
                    low,
                    weighted[core * 16 : core * 16 + 8, lanes],
                    weighted[core * 16 + 8 : core * 16 + 16, lanes],
                )
            value = solve(t, core, remain, NN_DIMS)
            fx[t, core] = value
            results.append(value)
        n = TLEV + t - 1
        if t > 0:
            xu[t - 1, 0, nz - 1] = jnp.concatenate(results, axis=0).astype(BF16)
            for p in range(nz - 1):
                seen = facing(p)
                g = 0 if seen < nfar else 1
                send(
                    xu.at[t - 1, 0, nz - 1],
                    xu.at[t - 1, 0, seen],
                    z_send.at[2 * n],
                    z_recv.at[2 * n + g],
                    z_peer(p),
                )

        osc[t, me] = fx[t, c]
        for j in range(1, cells):
            other, device = cell_peer(j)
            send(fx.at[t, other & 1], osc.at[t, me], f_send, f_recv.at[t], device)
        if t + 1 < LEVELS:
            finish(t + 1)

        if t > 0:

            def expand(j, p, t=t):
                value = xu[t - 1, j, p].astype(F32)
                slot = (t - 1) * cols + unit_of(j, p) * 4
                for h in range(2):
                    half = value[h * RW : (h + 1) * RW]
                    turned = pltpu.roll(half, BS, 1)
                    xs[slot + 2 * h] = jnp.where(low, half, turned)
                    xs[slot + 2 * h + 1] = jnp.where(low, turned, half)

            for g, (begin, end) in reversed(list(enumerate(groups))):
                count = min(end, nz - 1) - begin
                if count > 0:
                    settle(xu.at[t - 1, 0, pl.ds(begin, count)], z_recv.at[2 * n + g])
                there = pl.ds(begin, end - begin)
                for j in range(1, ny):
                    send(
                        xu.at[t - 1, 0, there],
                        xu.at[t - 1, ny - j, there],
                        y_send.at[2 * n + g],
                        y_recv.at[2 * n + g],
                        y_peer(j),
                    )
                for p in range(begin, end):
                    expand(0, p)
            for g, (begin, end) in reversed(list(enumerate(groups))):
                there = pl.ds(begin, end - begin)
                settle(xu.at[t - 1, pl.ds(1, ny - 1), there], y_recv.at[2 * n + g])

                @pl.loop(1, ny)
                def _(j, begin=begin, end=end):
                    for p in range(begin, end):
                        expand(j, p)

    finish(0)

    settle(trg.at[pl.ds(0, cells - 1)], cell_sem.at[0])
    settle(bu.at[0], cell_sem.at[2])
    settle(ddc.at[0], cell_sem.at[4])
    settle(p0r.at[pl.ds(0, cells - 1)], cell_sem.at[6])
    for t in range(TLEV):
        settle(pg.at[t, pl.ds(0, cells - 1)], pan_sem.at[0, t])
        settle(rz.at[t], z_send.at[2 * t])
        settle(xu.at[t, 0, pl.ds(0, nz - 1)], z_send.at[2 * (TLEV + t)])
        for g, (begin, end) in enumerate(groups):
            there = pl.ds(begin, end - begin)
            settle(ry.at[t, :, there], y_send.at[2 * t + g])
            settle(xu.at[t, pl.ds(1, ny - 1), there], y_send.at[2 * (TLEV + t) + g])
    for t in range(LEVELS):
        settle(osc.at[t, pl.ds(0, cells - 1)], f_send)


def pairs_of(value):
    value = value.reshape(LEVELS, BPL, -1, 128).transpose(0, 2, 1, 3)
    return value.reshape(LEVELS, -1, 128)


def local(right_side, diag_inverse, panels, tile_rows):
    owners = lax.axis_size("col")
    rows = lax.axis_size("row")
    ny, nz = sizes(owners)
    units = owners // 2
    cols = owners * BPL
    cells = 2 * rows
    chunks = (TLEV * cols + 127) // 128
    table_rows = 2 * TLEV + TLEV * chunks
    me = lax.axis_index("row") * 2 + lax.axis_index("col") % 2
    pan = panels.reshape(TLEV, BPL * BS, NNZ_DEV * BS)
    per = BPL * NNZ_DEV
    spread = jnp.tile(tile_rows.reshape(TLEV, per), (2, 128 // per))
    lane = lax.broadcasted_iota(jnp.int32, (8, 128), 1)
    tr = jnp.where(lane // per == me, spread, 0)
    if cells * per < 128:
        tr = jnp.where(lane >= cells * per, 1 << 20, tr)
    vmem = pl.BlockSpec(memory_space=pltpu.VMEM)
    result = pl.pallas_call(
        functools.partial(kernel, owners, rows),
        out_shape=jax.ShapeDtypeStruct((LEVELS, BS, 128), F32),
        in_specs=[vmem, vmem, vmem, pl.BlockSpec(memory_space=pl.ANY)],
        out_specs=vmem,
        scratch_shapes=[
            pltpu.VMEM((cells, 8, 128), jnp.int32),
            pltpu.VMEM((2 * LEVELS, 128, 128), F32),
            pltpu.VMEM((LEVELS, cells, RW, 128), F32),
            pltpu.VMEM((2, LEVELS, RW, 128), F32),
            pltpu.VMEM((2, LEVELS, 2, 128, 128), BF16),
            pltpu.VMEM((TLEV, cells, BPL * BS, NNZ_DEV * BS), BF16),
            pltpu.VMEM((cells, 2 * RW, NNZ_DEV * BS), BF16),
            pltpu.VMEM((cells, 2 * RW, NNZ_DEV * BS), BF16),
            pltpu.VMEM((table_rows, 128), jnp.int32),
            pltpu.VMEM((8, 128), F32),
            pltpu.SMEM((table_rows, 128), jnp.int32),
            pltpu.SMEM((8, 128), F32),
            pltpu.VMEM((128, RW, 128), F32),
            pltpu.VMEM((129, RW, 128), F32),
            pltpu.VMEM((TLEV - 1, units * 2, RW, 128), F32),
            pltpu.VMEM((TLEV, ny, nz, 2 * RW, 128), BF16),
            pltpu.VMEM((nz, 2, RW, 128), F32),
            pltpu.VMEM((TLEV, ny - 1, nz, 2 * RW, 128), BF16),
            pltpu.VMEM((TLEV, nz - 1, 2 * RW, 128), BF16),
            pltpu.VMEM((TLEV, nz - 1, 2 * RW, 128), BF16),
            pltpu.VMEM((LEVELS, 2, RW, 128), F32),
            pltpu.VMEM((TLEV, ny, nz, 2 * RW, 128), BF16),
            pltpu.VMEM((TLEV * cols, RW, 128), F32),
            pltpu.VMEM((LEVELS, 2, RW, 128), F32),
            pltpu.VMEM((LEVELS, cells, RW, 128), F32),
            pltpu.SemaphoreType.DMA((8,)),
            pltpu.SemaphoreType.DMA((2, TLEV)),
            pltpu.SemaphoreType.DMA((TLEV,)),
            pltpu.SemaphoreType.DMA((2,)),
            pltpu.SemaphoreType.DMA((4 * TLEV,)),
            pltpu.SemaphoreType.DMA((4 * TLEV,)),
            pltpu.SemaphoreType.DMA((4 * TLEV,)),
            pltpu.SemaphoreType.DMA((4 * TLEV,)),
            pltpu.SemaphoreType.DMA,
            pltpu.SemaphoreType.DMA((LEVELS,)),
        ],
        compiler_params=pltpu.CompilerParams(
            collective_id=0, has_side_effects=True, vmem_limit_bytes=40 * 1024 * 1024
        ),
    )(pairs_of(right_side), pairs_of(diag_inverse), tr, pan)
    result = result.reshape(LEVELS, -1, BPL, 128).transpose(0, 2, 1, 3)
    return result.reshape(LEVELS, BPL, -1)


def solution(mesh):
    in_specs = (
        P(None, "col", None),
        P(None, "col", None),
        P(None, "col", None, "row"),
        P(None, "col", "row"),
    )
    out_specs = P(None, "col", None)
    return jax.shard_map(local, mesh=mesh, in_specs=in_specs, out_specs=out_specs, check_vma=False)
```

```python
import functools

import jax
import jax.numpy as jnp
from jax import lax
from jax.experimental import pallas as pl
from jax.experimental.pallas import tpu as pltpu
from jax.sharding import PartitionSpec as P

BS = 64
LEVELS = 5
BPL = 2
NNZ_DEV = 8
TLEV = 4
RW = 8
MESH = pl.DeviceIdType.MESH
F32 = jnp.float32
BF16 = jnp.bfloat16
BOUNDS = (0, 3, 9, 16)
NT_DIMS = (((1,), (1,)), ((), ()))
NN_DIMS = (((1,), (0,)), ((), ()))


def sizes(owners):
    nz = 16 if owners % 32 == 0 else owners // 4
    return owners // 2 // nz, nz


def groups_of(nz):
    bounds = BOUNDS if nz == 16 else (0, max(1, nz // 2 - 1), nz)
    return tuple(zip(bounds[:-1], bounds[1:]))


def split(value):
    high = value.astype(BF16)
    return high, (value - high.astype(F32)).astype(BF16)


def product(value, pair, dims):
    rows = value.shape[0]
    high, rest = split(value)
    both = jnp.concatenate([high.astype(F32), rest.astype(F32)], axis=0).astype(BF16)
    first = lax.dot_general(both, pair[0], dims, preferred_element_type=F32)
    second = lax.dot_general(high, pair[1], dims, preferred_element_type=F32)
    return first[:rows] + (first[rows:] + second)


def kernel(
    owners,
    rows,
    rs_far,
    di_far,
    tr,
    pan,
    out,
    rs,
    di,
    trg,
    flip,
    bt,
    bu,
    ddc,
    pg,
    p0s,
    p0r,
    tbl,
    keepv,
    tbs,
    keeps,
    pd,
    cs,
    acc,
    sb,
    own,
    ry,
    sz,
    rz,
    ys,
    xu,
    xs,
    fx,
    osc,
    cell_sem,
    pan_sem,
    loc_sem,
    tab_sem,
    y_send,
    y_recv,
    z_send,
    z_recv,
    f_send,
    f_recv,
):
    ny, nz = sizes(owners)
    units = owners // 2
    cols = owners * BPL
    cells = 2 * rows
    per = BPL * NNZ_DEV
    tiles = cells * per
    chunks = (TLEV * cols + 127) // 128
    groups = groups_of(nz)
    parts = len(groups)
    col = lax.axis_index("col")
    x = lax.axis_index("row")
    c = col & 1
    z = (col // 2) & (nz - 1)
    y = col // (2 * nz)
    me = x * 2 + c

    def at(x_to, y_to, z_to, c_to):
        return {"row": x_to, "col": (y_to * nz + z_to) * 2 + c_to}

    def cell_peer(j):
        other = (me + j) & (cells - 1)
        return other, at(other // 2, y, z, other & 1)

    def y_peer(j):
        return at(x, (y + j) & (ny - 1), z, c)

    def step(p):
        half = (p + 1) // 2
        return nz // 2 + (half if p % 2 == 0 else -half)

    def facing(p):
        return p if step(p) in (0, nz // 2) else p + 1 if p % 2 == 1 else p - 1

    def z_peer(p):
        return at(x, y, (z + step(p)) & (nz - 1), c)

    def unit_of(j, p):
        return ((y + j) & (ny - 1)) * nz + ((z + step(p)) & (nz - 1))

    def send(src, dst, send_sem, recv_sem, device):
        pltpu.make_async_remote_copy(
            src_ref=src,
            dst_ref=dst,
            send_sem=send_sem,
            recv_sem=recv_sem,
            device_id=device,
            device_id_type=MESH,
        ).start()

    def settle(ref, sem):
        pltpu.make_async_copy(ref, ref, sem).wait()

    def low_of(count):
        return lax.broadcasted_iota(jnp.int32, (count, 128), 1) < BS

    low = low_of(RW)
    low32 = low_of(32)

    pltpu.make_async_copy(rs_far, rs, loc_sem.at[TLEV]).start()
    pltpu.make_async_copy(di_far, di, loc_sem.at[TLEV + 1]).start()
    pltpu.make_async_copy(tr, trg.at[me], loc_sem.at[TLEV + 2]).start()
    for t in range(TLEV):
        pltpu.make_async_copy(pan.at[t], pg.at[t, me], loc_sem.at[t]).start()

    barrier = pltpu.get_barrier_semaphore()

    def greet(device):
        pl.semaphore_signal(barrier, inc=1, device_id=device, device_id_type=MESH)

    for p in range(nz - 1):
        greet(z_peer(p))
    for j in range(1, ny):
        greet(y_peer(j))
    for j in range(1, cells):
        greet(cell_peer(j)[1])

    pltpu.make_async_copy(rs_far, rs, loc_sem.at[TLEV]).wait()
    pltpu.make_async_copy(di_far, di, loc_sem.at[TLEV + 1]).wait()
    pltpu.make_async_copy(tr, trg.at[me], loc_sem.at[TLEV + 2]).wait()
    for t in range(LEVELS):
        for k in range(BPL):
            value = rs[t, pl.ds(k, 32, 2), :]
            flip[t, pl.ds(k * BS, 32, 2), :] = value
            flip[t, pl.ds(k * BS + 1, 32, 2), :] = pltpu.roll(value, BS, 1)
            value = di[t, pl.ds(k, 32, 2), :]
            turned = pltpu.roll(value, BS, 1)
            keep = low32 if k == 0 else jnp.logical_not(low32)
            for par in range(2):
                half = value if par == k else turned
                flip[LEVELS + t, pl.ds(k * BS + par, 32, 2), :] = jnp.where(keep, half, 0.0)
    cells_r = cells * RW
    for t in range(LEVELS):
        turned = flip[t].T
        for q in range(cells):
            bt[t, q] = turned[q * RW : (q + 1) * RW]
        high, rest = split(flip[LEVELS + t])
        ddc[c, t, 0] = high
        ddc[c, t, 1] = rest
    for t in range(LEVELS):
        bu[c, t] = bt[t, me]

    right = bt[0].reshape(cells_r, 128)
    solved = product(right, (ddc[c, 0, 0], ddc[c, 0, 1]), NT_DIMS)
    pieces = []
    for q in range(cells):
        value = solved[q * RW : (q + 1) * RW]
        pieces += [jnp.where(low, value, 0.0), jnp.where(low, 0.0, value)]
    pltpu.make_async_copy(pan.at[0], pg.at[0, me], loc_sem.at[0]).wait()
    value = lax.dot_general(
        jnp.concatenate(pieces, axis=0).astype(BF16),
        pg[0, me],
        NN_DIMS,
        preferred_element_type=F32,
    ).astype(BF16)
    for q in range(cells):
        p0s[q] = value[q * 2 * RW : (q + 1) * 2 * RW]

    pl.semaphore_wait(barrier, cells - 1 + ny - 1 + nz - 1)

    for j in range(1, cells):
        other, device = cell_peer(j)
        send(tr, trg.at[me], cell_sem.at[0], cell_sem.at[1], device)
    for j in range(1, cells):
        other, device = cell_peer(j)
        send(p0s.at[other], p0r.at[me], cell_sem.at[6], cell_sem.at[7], device)
    core_peer = at(x, y, z, 1 - c)
    send(bt.at[:, me + 1 - 2 * c], bu.at[c], cell_sem.at[2], cell_sem.at[3], core_peer)
    send(ddc.at[c], ddc.at[c], cell_sem.at[4], cell_sem.at[5], core_peer)

    def send_panels(t):
        for j in range(1, cells):
            device = cell_peer(j)[1]
            send(pan.at[t], pg.at[t, me], pan_sem.at[0, t], pan_sem.at[1, t], device)

    send_panels(1)
    p0r[me] = p0s[me]

    settle(trg.at[pl.ds(0, cells - 1)], cell_sem.at[1])
    pieces = [trg[q, :, k, :] for q in range(cells) for k in range(BPL)]
    if tiles < 128:
        pieces.append(jnp.full((TLEV, 128 - tiles), 1 << 20, jnp.int32))
    targets = jnp.concatenate(pieces, axis=1)
    square = (128, 128)
    above = lax.broadcasted_iota(jnp.int32, square, 0)
    lane = lax.broadcasted_iota(jnp.int32, square, 1)
    for t in range(TLEV):
        mine = jnp.broadcast_to(targets[t : t + 1, :], square)
        other = mine.T
        before = (other < mine) | ((other == mine) & (above < lane))
        rank = jnp.sum(before.astype(jnp.int32), axis=0, keepdims=True)
        placed = jnp.broadcast_to(rank, square).T == lane
        order = jnp.sum(jnp.where(placed, above, 0), axis=0, keepdims=True)
        ordered = jnp.sum(jnp.where(placed, other, 0), axis=0, keepdims=True)
        ordered8 = jnp.broadcast_to(ordered, (8, 128))
        first = lax.broadcasted_iota(jnp.int32, (8, 128), 1) == 0
        same = (ordered8 == pltpu.roll(ordered8, 1, 1)) & jnp.logical_not(first)
        keepv[t : t + 1, :] = same.astype(F32)[0:1]
        tbl[t : t + 1, :] = order
        source = jnp.clip(mine[0:1] - cols, 0, TLEV * cols - 1)
        tbl[TLEV + t : TLEV + t + 1, :] = source
        for chunk in range(t * cols // 128, chunks):
            slot = lane + (cols + chunk * 128)
            upto = jnp.sum((other <= slot).astype(jnp.int32), axis=0, keepdims=True)
            equal = jnp.sum((other == slot).astype(jnp.int32), axis=0, keepdims=True)
            row = 2 * TLEV + t * chunks + chunk
            tbl[row : row + 1, :] = jnp.where(equal > 0, upto - 1, 128)
    pltpu.make_async_copy(tbl, tbs, tab_sem.at[0]).start()
    pltpu.make_async_copy(keepv, keeps, tab_sem.at[1]).start()
    pltpu.make_async_copy(tbl, tbs, tab_sem.at[0]).wait()
    pltpu.make_async_copy(keepv, keeps, tab_sem.at[1]).wait()
    cs[128] = jnp.zeros((RW, 128), F32)

    def halves_of(t, level, u):
        number = (level - 1) * cols + u * 4
        row = 2 * TLEV + t * chunks + lax.shift_right_logical(number, 7)
        place = number & 127
        parts = [cs[tbs[row, place + k]] for k in range(4)]
        halves = [jnp.where(low, parts[0], parts[1]), jnp.where(low, parts[2], parts[3])]
        if t > 0:
            halves = [halves[h] + acc[level - 2, u * 2 + h] for h in range(2)]
        return halves

    def tile_pair(tile, value):
        turned = pltpu.roll(value, BS, 1)
        pd[tile] = jnp.where(low, value, turned)
        pd[tile + 1] = jnp.where(low, turned, value)

    def solve(t, core, remain, dims):
        return product(remain, (ddc[core, t, 0], ddc[core, t, 1]), dims)

    def forward(t, update):
        solved = []
        for core in range(2):
            remain = bu[core, t]
            if update is not None:
                remain = remain - update[core]
            value = solve(t, core, remain, NT_DIMS)
            ys[t, core] = value
            solved.append(value)
        return solved

    update = None
    for t in range(TLEV):
        if t == 0:
            settle(p0r.at[pl.ds(0, cells - 1)], cell_sem.at[7])
            for q in range(cells):
                value = p0r[q].astype(F32)
                for k in range(2):
                    for p in range(4):
                        part = value[k * RW : (k + 1) * RW, p * 128 : (p + 1) * 128]
                        tile_pair(q * per + k * NNZ_DEV + p * 2, part)
        else:
            solved = forward(t, update)
            nothing = jnp.zeros((RW, 128), F32)
            pieces = []
            for core in range(2):
                for k in range(2):
                    kept = jnp.where(low, solved[core], 0.0)
                    if k == 1:
                        kept = jnp.where(low, 0.0, solved[core])
                    side = [kept, nothing] if core == 0 else [nothing, kept]
                    pieces.append(jnp.concatenate(side, axis=1))
            vectors = jnp.concatenate(pieces, axis=0).astype(BF16)
            settle(pg.at[t, 0], loc_sem.at[t])
            settle(pg.at[t, pl.ds(0, cells - 1)], pan_sem.at[1, t])
            for group in range(rows):
                panel = pg[t, pl.ds(2 * group, 2)].reshape(4 * BS, NNZ_DEV * BS)
                value = lax.dot_general(vectors, panel, NN_DIMS, preferred_element_type=F32)
                for b in range(4):
                    for p in range(4):
                        part = value[b * RW : (b + 1) * RW, p * 128 : (p + 1) * 128]
                        tile_pair(group * 32 + b * 8 + p * 2, part)

        def scan(i, total, t=t):
            for k in range(16):
                place = i * 16 + k
                total = total * keeps[t, place] + pd[tbs[t, place]]
                cs[place] = total
            return total

        lax.fori_loop(0, tiles // 16, scan, jnp.zeros((RW, 128), F32))

        for g, (begin, end) in enumerate(groups):

            @pl.loop(0, ny - 1)
            def _(i, t=t, g=g, begin=begin, end=end):
                j = jnp.where(i == 0, ny // 2, jnp.where(i < ny // 2 + (ny == 2), i, i + 1))
                for p in range(begin, end):
                    halves = halves_of(t, t + 1, unit_of(j, p))
                    sb[t, j, p] = jnp.concatenate(halves, axis=0).astype(BF16)
                there = pl.ds(begin, end - begin)
                send(
                    sb.at[t, j, there],
                    ry.at[t, j - 1, there],
                    y_send.at[parts * t + g],
                    y_recv.at[parts * t + g],
                    y_peer(j),
                )

        for p in range(nz):
            halves = halves_of(t, t + 1, unit_of(0, p))
            own[p, 0] = halves[0]
            own[p, 1] = halves[1]
        if t + 2 < TLEV:
            send_panels(t + 2)
        for level in range(t + 2, LEVELS):

            @pl.loop(0, units // 4)
            def _(i, t=t, level=level):
                for k in range(4):
                    u = i * 4 + k
                    halves = halves_of(t, level, u)
                    acc[level - 2, u * 2] = halves[0]
                    acc[level - 2, u * 2 + 1] = halves[1]

        if t == 0:
            settle(bu.at[0], cell_sem.at[3])
            settle(ddc.at[0], cell_sem.at[5])
            forward(0, None)

        def partial(p, t=t):
            halves = []
            for h in range(2):
                value = own[p, h]
                for j in range(ny - 1):
                    value = value + ry[t, j, p].astype(F32)[h * RW : (h + 1) * RW]
                halves.append(value)
            return halves

        for g, (begin, end) in enumerate(groups):
            settle(ry.at[t, :, pl.ds(begin, end - begin)], y_recv.at[parts * t + g])
            for p in range(begin, min(end, nz - 1)):
                sz[t, p] = jnp.concatenate(partial(p), axis=0).astype(BF16)
                send(sz.at[t, p], rz.at[t, p], z_send.at[parts * t], z_recv.at[parts * t], z_peer(p))
        update = partial(nz - 1)
        settle(rz.at[t], z_recv.at[parts * t])
        for p in range(nz - 1):
            arrived = rz[t, p].astype(F32)
            update = [update[0] + arrived[:RW], update[1] + arrived[RW:]]

    send_panels(0)
    forward(TLEV, update)

    def finish(t):
        settle(osc.at[t, pl.ds(0, cells - 1)], f_recv.at[t])
        value = osc[t].reshape(cells_r, 128)
        if cells_r < 128:
            value = jnp.concatenate([value] * (128 // cells_r), axis=0)
        flip[t] = value.T
        for k in range(BPL):
            even = flip[t, pl.ds(k * BS, 32, 2), :]
            odd = flip[t, pl.ds(k * BS + 1, 32, 2), :]
            out[t, pl.ds(k, 32, 2), :] = jnp.where(low32, even, odd)

    for t in range(LEVELS - 1, -1, -1):
        if t < TLEV:
            if t == 0:
                settle(pg.at[0, pl.ds(0, cells - 1)], pan_sem.at[1, 0])
            weighted = None
            for group in range(rows):
                lines = []
                for b in range(4):
                    line = []
                    for p in range(4):
                        tile = group * 32 + b * 8 + p * 2
                        first = xs[tbs[TLEV + t, tile]]
                        second = xs[tbs[TLEV + t, tile + 1]]
                        line.append(jnp.where(low, first, second))
                    lines.append(jnp.concatenate(line, axis=1))
                picked = jnp.concatenate(lines, axis=0).astype(BF16)
                panel = pg[t, pl.ds(2 * group, 2)].reshape(4 * BS, NNZ_DEV * BS)
                value = lax.dot_general(picked, panel, NT_DIMS, preferred_element_type=F32)
                weighted = value if weighted is None else weighted + value
        results = []
        for core in range(2):
            remain = ys[t, core]
            if t < TLEV:
                lanes = slice(core * 128, core * 128 + 128)
                remain = remain - jnp.where(
                    low,
                    weighted[core * 16 : core * 16 + 8, lanes],
                    weighted[core * 16 + 8 : core * 16 + 16, lanes],
                )
            value = solve(t, core, remain, NN_DIMS)
            fx[t, core] = value
            results.append(value)
        n = TLEV + t - 1
        if t > 0:
            xu[t - 1, 0, nz - 1] = jnp.concatenate(results, axis=0).astype(BF16)
            for p in range(nz - 1):
                seen = facing(p)
                g = [begin <= seen < end for begin, end in groups].index(True)
                send(
                    xu.at[t - 1, 0, nz - 1],
                    xu.at[t - 1, 0, seen],
                    z_send.at[parts * n],
                    z_recv.at[parts * n + g],
                    z_peer(p),
                )

        osc[t, me] = fx[t, c]
        for j in range(1, cells):
            other, device = cell_peer(j)
            send(fx.at[t, other & 1], osc.at[t, me], f_send, f_recv.at[t], device)
        if t + 1 < LEVELS:
            finish(t + 1)

        if t > 0:

            def expand(j, p, t=t):
                value = xu[t - 1, j, p].astype(F32)
                slot = (t - 1) * cols + unit_of(j, p) * 4
                for h in range(2):
                    half = value[h * RW : (h + 1) * RW]
                    turned = pltpu.roll(half, BS, 1)
                    xs[slot + 2 * h] = jnp.where(low, half, turned)
                    xs[slot + 2 * h + 1] = jnp.where(low, turned, half)

            for g, (begin, end) in reversed(list(enumerate(groups))):
                count = min(end, nz - 1) - begin
                if count > 0:
                    settle(xu.at[t - 1, 0, pl.ds(begin, count)], z_recv.at[parts * n + g])
                there = pl.ds(begin, end - begin)
                for j in range(1, ny):
                    send(
                        xu.at[t - 1, 0, there],
                        xu.at[t - 1, ny - j, there],
                        y_send.at[parts * n + g],
                        y_recv.at[parts * n + g],
                        y_peer(j),
                    )
                for p in range(begin, end):
                    expand(0, p)
            for g, (begin, end) in reversed(list(enumerate(groups))):
                there = pl.ds(begin, end - begin)
                settle(xu.at[t - 1, pl.ds(1, ny - 1), there], y_recv.at[parts * n + g])

                @pl.loop(1, ny)
                def _(j, begin=begin, end=end):
                    for p in range(begin, end):
                        expand(j, p)

    finish(0)

    settle(trg.at[pl.ds(0, cells - 1)], cell_sem.at[0])
    settle(bu.at[0], cell_sem.at[2])
    settle(ddc.at[0], cell_sem.at[4])
    settle(p0r.at[pl.ds(0, cells - 1)], cell_sem.at[6])
    for t in range(TLEV):
        settle(pg.at[t, pl.ds(0, cells - 1)], pan_sem.at[0, t])
        settle(rz.at[t], z_send.at[parts * t])
        settle(xu.at[t, 0, pl.ds(0, nz - 1)], z_send.at[parts * (TLEV + t)])
        for g, (begin, end) in enumerate(groups):
            there = pl.ds(begin, end - begin)
            settle(ry.at[t, :, there], y_send.at[parts * t + g])
            settle(xu.at[t, pl.ds(1, ny - 1), there], y_send.at[parts * (TLEV + t) + g])
    for t in range(LEVELS):
        settle(osc.at[t, pl.ds(0, cells - 1)], f_send)


def pairs_of(value):
    value = value.reshape(LEVELS, BPL, -1, 128).transpose(0, 2, 1, 3)
    return value.reshape(LEVELS, -1, 128)


def local(right_side, diag_inverse, panels, tile_rows):
    owners = lax.axis_size("col")
    rows = lax.axis_size("row")
    ny, nz = sizes(owners)
    parts = len(groups_of(nz))
    units = owners // 2
    cols = owners * BPL
    cells = 2 * rows
    chunks = (TLEV * cols + 127) // 128
    table_rows = 2 * TLEV + TLEV * chunks
    pan = panels.reshape(TLEV, BPL * BS, NNZ_DEV * BS)
    vmem = pl.BlockSpec(memory_space=pltpu.VMEM)
    far = pl.BlockSpec(memory_space=pltpu.HBM)
    result = pl.pallas_call(
        functools.partial(kernel, owners, rows),
        out_shape=jax.ShapeDtypeStruct((LEVELS, BS, 128), F32),
        in_specs=[far, far, far, far],
        out_specs=vmem,
        scratch_shapes=[
            pltpu.VMEM((LEVELS, BS, 128), F32),
            pltpu.VMEM((LEVELS, BS, 128), F32),
            pltpu.VMEM((cells, TLEV, BPL, NNZ_DEV), jnp.int32),
            pltpu.VMEM((2 * LEVELS, 128, 128), F32),
            pltpu.VMEM((LEVELS, cells, RW, 128), F32),
            pltpu.VMEM((2, LEVELS, RW, 128), F32),
            pltpu.VMEM((2, LEVELS, 2, 128, 128), BF16),
            pltpu.VMEM((TLEV, cells, BPL * BS, NNZ_DEV * BS), BF16),
            pltpu.VMEM((cells, 2 * RW, NNZ_DEV * BS), BF16),
            pltpu.VMEM((cells, 2 * RW, NNZ_DEV * BS), BF16),
            pltpu.VMEM((table_rows, 128), jnp.int32),
            pltpu.VMEM((8, 128), F32),
            pltpu.SMEM((table_rows, 128), jnp.int32),
            pltpu.SMEM((8, 128), F32),
            pltpu.VMEM((128, RW, 128), F32),
            pltpu.VMEM((129, RW, 128), F32),
            pltpu.VMEM((TLEV - 1, units * 2, RW, 128), F32),
            pltpu.VMEM((TLEV, ny, nz, 2 * RW, 128), BF16),
            pltpu.VMEM((nz, 2, RW, 128), F32),
            pltpu.VMEM((TLEV, ny - 1, nz, 2 * RW, 128), BF16),
            pltpu.VMEM((TLEV, nz - 1, 2 * RW, 128), BF16),
            pltpu.VMEM((TLEV, nz - 1, 2 * RW, 128), BF16),
            pltpu.VMEM((LEVELS, 2, RW, 128), F32),
            pltpu.VMEM((TLEV, ny, nz, 2 * RW, 128), BF16),
            pltpu.VMEM((TLEV * cols, RW, 128), F32),
            pltpu.VMEM((LEVELS, 2, RW, 128), F32),
            pltpu.VMEM((LEVELS, cells, RW, 128), F32),
            pltpu.SemaphoreType.DMA((8,)),
            pltpu.SemaphoreType.DMA((2, TLEV)),
            pltpu.SemaphoreType.DMA((TLEV + 3,)),
            pltpu.SemaphoreType.DMA((2,)),
            pltpu.SemaphoreType.DMA((2 * TLEV * parts,)),
            pltpu.SemaphoreType.DMA((2 * TLEV * parts,)),
            pltpu.SemaphoreType.DMA((2 * TLEV * parts,)),
            pltpu.SemaphoreType.DMA((2 * TLEV * parts,)),
            pltpu.SemaphoreType.DMA,
            pltpu.SemaphoreType.DMA((LEVELS,)),
        ],
        compiler_params=pltpu.CompilerParams(
            collective_id=0, has_side_effects=True, vmem_limit_bytes=58 * 1024 * 1024
        ),
    )(pairs_of(right_side), pairs_of(diag_inverse), tile_rows, pan)
    result = result.reshape(LEVELS, -1, BPL, 128).transpose(0, 2, 1, 3)
    return result.reshape(LEVELS, BPL, -1)


def solution(mesh):
    in_specs = (
        P(None, "col", None),
        P(None, "col", None),
        P(None, "col", None, "row"),
        P(None, "col", "row"),
    )
    out_specs = P(None, "col", None)
    return jax.shard_map(local, mesh=mesh, in_specs=in_specs, out_specs=out_specs, check_vma=False)
```

```python
import functools

import jax
import jax.numpy as jnp
from jax import lax
from jax.experimental import pallas as pl
from jax.experimental.pallas import tpu as pltpu
from jax.sharding import PartitionSpec as P

BS = 64
LEVELS = 5
BPL = 2
NNZ_DEV = 8
TLEV = 4
RW = 8
MESH = pl.DeviceIdType.MESH
F32 = jnp.float32
BF16 = jnp.bfloat16
BOUNDS = (0, 3, 9, 16)
NT_DIMS = (((1,), (1,)), ((), ()))
NN_DIMS = (((1,), (0,)), ((), ()))


def sizes(owners):
    nz = 16 if owners % 32 == 0 else owners // 4
    return owners // 2 // nz, nz


def groups_of(nz):
    bounds = BOUNDS if nz == 16 else (0, max(1, nz // 2 - 1), nz)
    return tuple(zip(bounds[:-1], bounds[1:]))


def split(value):
    high = value.astype(BF16)
    return high, (value - high.astype(F32)).astype(BF16)


def product(value, pair, dims):
    rows = value.shape[0]
    high, rest = split(value)
    both = jnp.concatenate([high.astype(F32), rest.astype(F32)], axis=0).astype(BF16)
    first = lax.dot_general(both, pair[0], dims, preferred_element_type=F32)
    second = lax.dot_general(high, pair[1], dims, preferred_element_type=F32)
    return first[:rows] + (first[rows:] + second)


def kernel(
    owners,
    rows,
    rs_far,
    di_far,
    tr,
    pan,
    out,
    rs,
    di,
    trg,
    flip,
    bt,
    bu,
    ddc,
    pg,
    p0s,
    p0r,
    tbl,
    keepv,
    tbs,
    keeps,
    pd,
    cs,
    acc,
    sb,
    own,
    ry,
    sz,
    rz,
    ys,
    xu,
    xs,
    fx,
    osc,
    cell_sem,
    pan_sem,
    loc_sem,
    tab_sem,
    y_send,
    y_recv,
    z_send,
    z_recv,
    f_send,
    f_recv,
):
    ny, nz = sizes(owners)
    units = owners // 2
    cols = owners * BPL
    cells = 2 * rows
    per = BPL * NNZ_DEV
    tiles = cells * per
    chunks = (TLEV * cols + 127) // 128
    groups = groups_of(nz)
    parts = len(groups)
    col = lax.axis_index("col")
    x = lax.axis_index("row")
    c = col & 1
    z = (col // 2) & (nz - 1)
    y = col // (2 * nz)
    me = x * 2 + c

    def at(x_to, y_to, z_to, c_to):
        return {"row": x_to, "col": (y_to * nz + z_to) * 2 + c_to}

    def cell_peer(j):
        other = (me + j) & (cells - 1)
        return other, at(other // 2, y, z, other & 1)

    def y_peer(j):
        return at(x, (y + j) & (ny - 1), z, c)

    def step(p):
        half = (p + 1) // 2
        return nz // 2 + (half if p % 2 == 0 else -half)

    def facing(p):
        return p if step(p) in (0, nz // 2) else p + 1 if p % 2 == 1 else p - 1

    def z_peer(p):
        return at(x, y, (z + step(p)) & (nz - 1), c)

    def unit_of(j, p):
        return ((y + j) & (ny - 1)) * nz + ((z + step(p)) & (nz - 1))

    def send(src, dst, send_sem, recv_sem, device):
        pltpu.make_async_remote_copy(
            src_ref=src,
            dst_ref=dst,
            send_sem=send_sem,
            recv_sem=recv_sem,
            device_id=device,
            device_id_type=MESH,
        ).start()

    def settle(ref, sem):
        pltpu.make_async_copy(ref, ref, sem).wait()

    def low_of(count):
        return lax.broadcasted_iota(jnp.int32, (count, 128), 1) < BS

    low = low_of(RW)
    low32 = low_of(32)

    pltpu.make_async_copy(rs_far, rs, loc_sem.at[TLEV]).start()
    pltpu.make_async_copy(di_far, di, loc_sem.at[TLEV + 1]).start()
    pltpu.make_async_copy(tr, trg.at[me], loc_sem.at[TLEV + 2]).start()
    for t in range(TLEV):
        pltpu.make_async_copy(pan.at[t], pg.at[t, me], loc_sem.at[t]).start()

    barrier = pltpu.get_barrier_semaphore()

    def greet(device):
        pl.semaphore_signal(barrier, inc=1, device_id=device, device_id_type=MESH)

    for p in range(nz - 1):
        greet(z_peer(p))
    for j in range(1, ny):
        greet(y_peer(j))
    for j in range(1, cells):
        greet(cell_peer(j)[1])

    pltpu.make_async_copy(rs_far, rs, loc_sem.at[TLEV]).wait()
    pltpu.make_async_copy(di_far, di, loc_sem.at[TLEV + 1]).wait()
    pltpu.make_async_copy(tr, trg.at[me], loc_sem.at[TLEV + 2]).wait()
    for t in range(LEVELS):
        for k in range(BPL):
            value = rs[t, pl.ds(k, 32, 2), :]
            flip[t, pl.ds(k * BS, 32, 2), :] = value
            flip[t, pl.ds(k * BS + 1, 32, 2), :] = pltpu.roll(value, BS, 1)
            value = di[t, pl.ds(k, 32, 2), :]
            turned = pltpu.roll(value, BS, 1)
            keep = low32 if k == 0 else jnp.logical_not(low32)
            for par in range(2):
                half = value if par == k else turned
                flip[LEVELS + t, pl.ds(k * BS + par, 32, 2), :] = jnp.where(keep, half, 0.0)
    cells_r = cells * RW
    for t in range(LEVELS):
        turned = flip[t].T
        for q in range(cells):
            bt[t, q] = turned[q * RW : (q + 1) * RW]
        high, rest = split(flip[LEVELS + t])
        ddc[c, t, 0] = high
        ddc[c, t, 1] = rest
    for t in range(LEVELS):
        bu[c, t] = bt[t, me]

    right = bt[0].reshape(cells_r, 128)
    solved = product(right, (ddc[c, 0, 0], ddc[c, 0, 1]), NT_DIMS)
    pieces = []
    for q in range(cells):
        value = solved[q * RW : (q + 1) * RW]
        pieces += [jnp.where(low, value, 0.0), jnp.where(low, 0.0, value)]
    pltpu.make_async_copy(pan.at[0], pg.at[0, me], loc_sem.at[0]).wait()
    value = lax.dot_general(
        jnp.concatenate(pieces, axis=0).astype(BF16),
        pg[0, me],
        NN_DIMS,
        preferred_element_type=F32,
    ).astype(BF16)
    for q in range(cells):
        p0s[q] = value[q * 2 * RW : (q + 1) * 2 * RW]

    pl.semaphore_wait(barrier, cells - 1 + ny - 1 + nz - 1)

    for j in range(1, cells):
        other, device = cell_peer(j)
        send(tr, trg.at[me], cell_sem.at[0], cell_sem.at[1], device)
    for j in range(1, cells):
        other, device = cell_peer(j)
        send(p0s.at[other], p0r.at[me], cell_sem.at[6], cell_sem.at[7], device)
    core_peer = at(x, y, z, 1 - c)
    send(bt.at[:, me + 1 - 2 * c], bu.at[c], cell_sem.at[2], cell_sem.at[3], core_peer)
    send(ddc.at[c], ddc.at[c], cell_sem.at[4], cell_sem.at[5], core_peer)

    def send_panels(t):
        for j in range(1, cells):
            device = cell_peer(j)[1]
            send(pan.at[t], pg.at[t, me], pan_sem.at[0, t], pan_sem.at[1, t], device)

    send_panels(1)
    p0r[me] = p0s[me]

    settle(trg.at[pl.ds(0, cells - 1)], cell_sem.at[1])
    pieces = [trg[q, :, k, :] for q in range(cells) for k in range(BPL)]
    if tiles < 128:
        pieces.append(jnp.full((TLEV, 128 - tiles), 1 << 20, jnp.int32))
    targets = jnp.concatenate(pieces, axis=1)
    square = (128, 128)
    above = lax.broadcasted_iota(jnp.int32, square, 0)
    lane = lax.broadcasted_iota(jnp.int32, square, 1)
    def table(t):
        mine = jnp.broadcast_to(targets[t : t + 1, :], square)
        other = mine.T
        before = (other < mine) | ((other == mine) & (above < lane))
        rank = jnp.sum(before.astype(jnp.int32), axis=0, keepdims=True)
        placed = jnp.broadcast_to(rank, square).T == lane
        order = jnp.sum(jnp.where(placed, above, 0), axis=0, keepdims=True)
        ordered = jnp.sum(jnp.where(placed, other, 0), axis=0, keepdims=True)
        ordered8 = jnp.broadcast_to(ordered, (8, 128))
        first = lax.broadcasted_iota(jnp.int32, (8, 128), 1) == 0
        same = (ordered8 == pltpu.roll(ordered8, 1, 1)) & jnp.logical_not(first)
        keepv[t, 0:1, :] = same.astype(F32)[0:1]
        tbl[t, 0:1, :] = order
        source = jnp.clip(mine[0:1] - cols, 0, TLEV * cols - 1)
        tbl[t, 1:2, :] = source
        for chunk in range(t * cols // 128, chunks):
            slot = lane + (cols + chunk * 128)
            upto = jnp.sum((other <= slot).astype(jnp.int32), axis=0, keepdims=True)
            equal = jnp.sum((other == slot).astype(jnp.int32), axis=0, keepdims=True)
            tbl[t, 2 + chunk : 3 + chunk, :] = jnp.where(equal > 0, upto - 1, 128)
        pltpu.make_async_copy(tbl.at[t], tbs.at[t], tab_sem.at[0]).start()
        pltpu.make_async_copy(keepv.at[t], keeps.at[t], tab_sem.at[1]).start()
        pltpu.make_async_copy(tbl.at[t], tbs.at[t], tab_sem.at[0]).wait()
        pltpu.make_async_copy(keepv.at[t], keeps.at[t], tab_sem.at[1]).wait()

    table(0)
    cs[128] = jnp.zeros((RW, 128), F32)

    def halves_of(t, level, u):
        number = (level - 1) * cols + u * 4
        row = 2 + lax.shift_right_logical(number, 7)
        place = number & 127
        found = [cs[tbs[t, row, place + k]] for k in range(4)]
        halves = [jnp.where(low, found[0], found[1]), jnp.where(low, found[2], found[3])]
        if t > 0:
            halves = [halves[h] + acc[level - 2, u * 2 + h] for h in range(2)]
        return halves

    def tile_pair(tile, value):
        turned = pltpu.roll(value, BS, 1)
        pd[tile] = jnp.where(low, value, turned)
        pd[tile + 1] = jnp.where(low, turned, value)

    def solve(t, core, remain, dims):
        return product(remain, (ddc[core, t, 0], ddc[core, t, 1]), dims)

    def forward(t, update):
        solved = []
        for core in range(2):
            remain = bu[core, t]
            if update is not None:
                remain = remain - update[core]
            value = solve(t, core, remain, NT_DIMS)
            ys[t, core] = value
            solved.append(value)
        return solved

    update = None
    for t in range(TLEV):
        if t == 0:
            settle(p0r.at[pl.ds(0, cells - 1)], cell_sem.at[7])
            for q in range(cells):
                value = p0r[q].astype(F32)
                for k in range(2):
                    for p in range(4):
                        part = value[k * RW : (k + 1) * RW, p * 128 : (p + 1) * 128]
                        tile_pair(q * per + k * NNZ_DEV + p * 2, part)
        else:
            solved = forward(t, update)
            nothing = jnp.zeros((RW, 128), F32)
            pieces = []
            for core in range(2):
                for k in range(2):
                    kept = jnp.where(low, solved[core], 0.0)
                    if k == 1:
                        kept = jnp.where(low, 0.0, solved[core])
                    side = [kept, nothing] if core == 0 else [nothing, kept]
                    pieces.append(jnp.concatenate(side, axis=1))
            vectors = jnp.concatenate(pieces, axis=0).astype(BF16)
            settle(pg.at[t, 0], loc_sem.at[t])
            settle(pg.at[t, pl.ds(0, cells - 1)], pan_sem.at[1, t])
            for group in range(rows):
                panel = pg[t, pl.ds(2 * group, 2)].reshape(4 * BS, NNZ_DEV * BS)
                value = lax.dot_general(vectors, panel, NN_DIMS, preferred_element_type=F32)
                for b in range(4):
                    for p in range(4):
                        part = value[b * RW : (b + 1) * RW, p * 128 : (p + 1) * 128]
                        tile_pair(group * 32 + b * 8 + p * 2, part)

        def scan(i, total, t=t):
            for k in range(16):
                place = i * 16 + k
                total = total * keeps[t, 0, place] + pd[tbs[t, 0, place]]
                cs[place] = total
            return total

        lax.fori_loop(0, tiles // 16, scan, jnp.zeros((RW, 128), F32))

        for g, (begin, end) in enumerate(groups):

            @pl.loop(0, ny - 1)
            def _(i, t=t, g=g, begin=begin, end=end):
                j = jnp.where(i == 0, ny // 2, jnp.where(i < ny // 2 + (ny == 2), i, i + 1))
                for p in range(begin, end):
                    halves = halves_of(t, t + 1, unit_of(j, p))
                    sb[t, j, p] = jnp.concatenate(halves, axis=0).astype(BF16)
                there = pl.ds(begin, end - begin)
                send(
                    sb.at[t, j, there],
                    ry.at[t, j - 1, there],
                    y_send.at[parts * t + g],
                    y_recv.at[parts * t + g],
                    y_peer(j),
                )

        for p in range(nz):
            halves = halves_of(t, t + 1, unit_of(0, p))
            own[p, 0] = halves[0]
            own[p, 1] = halves[1]
        def partial(p, t=t):
            halves = []
            for h in range(2):
                value = own[p, h]
                for j in range(ny - 1):
                    value = value + ry[t, j, p].astype(F32)[h * RW : (h + 1) * RW]
                halves.append(value)
            return halves

        for g, (begin, end) in enumerate(groups):
            settle(ry.at[t, :, pl.ds(begin, end - begin)], y_recv.at[parts * t + g])
            for p in range(begin, min(end, nz - 1)):
                sz[t, p] = jnp.concatenate(partial(p), axis=0).astype(BF16)
                send(
                    sz.at[t, p],
                    rz.at[t, p],
                    z_send.at[parts * t],
                    z_recv.at[parts * t + g],
                    z_peer(p),
                )
        if t + 2 < TLEV:
            send_panels(t + 2)
        for level in range(t + 2, LEVELS):

            @pl.loop(0, units // 4)
            def _(i, t=t, level=level):
                for k in range(4):
                    u = i * 4 + k
                    halves = halves_of(t, level, u)
                    acc[level - 2, u * 2] = halves[0]
                    acc[level - 2, u * 2 + 1] = halves[1]

        if t == 0:
            settle(bu.at[0], cell_sem.at[3])
            settle(ddc.at[0], cell_sem.at[5])
            forward(0, None)
        if t + 1 < TLEV:
            table(t + 1)

        update = partial(nz - 1)
        for g, (begin, end) in reversed(list(enumerate(groups))):
            count = min(end, nz - 1) - begin
            if count > 0:
                settle(rz.at[t, pl.ds(begin, count)], z_recv.at[parts * t + g])
            for p in range(begin, begin + count):
                arrived = rz[t, p].astype(F32)
                update = [update[0] + arrived[:RW], update[1] + arrived[RW:]]

    send_panels(0)
    forward(TLEV, update)

    def finish(t):
        settle(osc.at[t, pl.ds(0, cells - 1)], f_recv.at[t])
        value = osc[t].reshape(cells_r, 128)
        if cells_r < 128:
            value = jnp.concatenate([value] * (128 // cells_r), axis=0)
        flip[t] = value.T
        for k in range(BPL):
            even = flip[t, pl.ds(k * BS, 32, 2), :]
            odd = flip[t, pl.ds(k * BS + 1, 32, 2), :]
            out[t, pl.ds(k, 32, 2), :] = jnp.where(low32, even, odd)

    for t in range(LEVELS - 1, -1, -1):
        if t < TLEV:
            if t == 0:
                settle(pg.at[0, pl.ds(0, cells - 1)], pan_sem.at[1, 0])
            weighted = None
            for group in range(rows):
                lines = []
                for b in range(4):
                    line = []
                    for p in range(4):
                        tile = group * 32 + b * 8 + p * 2
                        first = xs[tbs[t, 1, tile]]
                        second = xs[tbs[t, 1, tile + 1]]
                        line.append(jnp.where(low, first, second))
                    lines.append(jnp.concatenate(line, axis=1))
                picked = jnp.concatenate(lines, axis=0).astype(BF16)
                panel = pg[t, pl.ds(2 * group, 2)].reshape(4 * BS, NNZ_DEV * BS)
                value = lax.dot_general(picked, panel, NT_DIMS, preferred_element_type=F32)
                weighted = value if weighted is None else weighted + value
        results = []
        for core in range(2):
            remain = ys[t, core]
            if t < TLEV:
                lanes = slice(core * 128, core * 128 + 128)
                remain = remain - jnp.where(
                    low,
                    weighted[core * 16 : core * 16 + 8, lanes],
                    weighted[core * 16 + 8 : core * 16 + 16, lanes],
                )
            value = solve(t, core, remain, NN_DIMS)
            fx[t, core] = value
            results.append(value)
        n = TLEV + t - 1
        if t > 0:
            xu[t - 1, 0, nz - 1] = jnp.concatenate(results, axis=0).astype(BF16)
            for p in range(nz - 1):
                seen = facing(p)
                g = [begin <= seen < end for begin, end in groups].index(True)
                send(
                    xu.at[t - 1, 0, nz - 1],
                    xu.at[t - 1, 0, seen],
                    z_send.at[parts * n],
                    z_recv.at[parts * n + g],
                    z_peer(p),
                )

        osc[t, me] = fx[t, c]
        for j in range(1, cells):
            other, device = cell_peer(j)
            send(fx.at[t, other & 1], osc.at[t, me], f_send, f_recv.at[t], device)
        if t + 1 < LEVELS:
            finish(t + 1)

        if t > 0:

            def expand(j, p, t=t):
                value = xu[t - 1, j, p].astype(F32)
                slot = (t - 1) * cols + unit_of(j, p) * 4
                for h in range(2):
                    half = value[h * RW : (h + 1) * RW]
                    turned = pltpu.roll(half, BS, 1)
                    xs[slot + 2 * h] = jnp.where(low, half, turned)
                    xs[slot + 2 * h + 1] = jnp.where(low, turned, half)

            for g, (begin, end) in reversed(list(enumerate(groups))):
                count = min(end, nz - 1) - begin
                if count > 0:
                    settle(xu.at[t - 1, 0, pl.ds(begin, count)], z_recv.at[parts * n + g])
                there = pl.ds(begin, end - begin)
                for j in range(1, ny):
                    send(
                        xu.at[t - 1, 0, there],
                        xu.at[t - 1, ny - j, there],
                        y_send.at[parts * n + g],
                        y_recv.at[parts * n + g],
                        y_peer(j),
                    )
                for p in range(begin, end):
                    expand(0, p)
            for g, (begin, end) in reversed(list(enumerate(groups))):
                there = pl.ds(begin, end - begin)
                settle(xu.at[t - 1, pl.ds(1, ny - 1), there], y_recv.at[parts * n + g])

                @pl.loop(1, ny)
                def _(j, begin=begin, end=end):
                    for p in range(begin, end):
                        expand(j, p)

    finish(0)

    settle(trg.at[pl.ds(0, cells - 1)], cell_sem.at[0])
    settle(bu.at[0], cell_sem.at[2])
    settle(ddc.at[0], cell_sem.at[4])
    settle(p0r.at[pl.ds(0, cells - 1)], cell_sem.at[6])
    for t in range(TLEV):
        settle(pg.at[t, pl.ds(0, cells - 1)], pan_sem.at[0, t])
        settle(rz.at[t], z_send.at[parts * t])
        settle(xu.at[t, 0, pl.ds(0, nz - 1)], z_send.at[parts * (TLEV + t)])
        for g, (begin, end) in enumerate(groups):
            there = pl.ds(begin, end - begin)
            settle(ry.at[t, :, there], y_send.at[parts * t + g])
            settle(xu.at[t, pl.ds(1, ny - 1), there], y_send.at[parts * (TLEV + t) + g])
    for t in range(LEVELS):
        settle(osc.at[t, pl.ds(0, cells - 1)], f_send)


def pairs_of(value):
    value = value.reshape(LEVELS, BPL, -1, 128).transpose(0, 2, 1, 3)
    return value.reshape(LEVELS, -1, 128)


def local(right_side, diag_inverse, panels, tile_rows):
    owners = lax.axis_size("col")
    rows = lax.axis_size("row")
    ny, nz = sizes(owners)
    parts = len(groups_of(nz))
    units = owners // 2
    cols = owners * BPL
    cells = 2 * rows
    chunks = (TLEV * cols + 127) // 128
    table_rows = (2 + chunks + 7) // 8 * 8
    pan = panels.reshape(TLEV, BPL * BS, NNZ_DEV * BS)
    vmem = pl.BlockSpec(memory_space=pltpu.VMEM)
    far = pl.BlockSpec(memory_space=pltpu.HBM)
    result = pl.pallas_call(
        functools.partial(kernel, owners, rows),
        out_shape=jax.ShapeDtypeStruct((LEVELS, BS, 128), F32),
        in_specs=[far, far, far, far],
        out_specs=vmem,
        scratch_shapes=[
            pltpu.VMEM((LEVELS, BS, 128), F32),
            pltpu.VMEM((LEVELS, BS, 128), F32),
            pltpu.VMEM((cells, TLEV, BPL, NNZ_DEV), jnp.int32),
            pltpu.VMEM((2 * LEVELS, 128, 128), F32),
            pltpu.VMEM((LEVELS, cells, RW, 128), F32),
            pltpu.VMEM((2, LEVELS, RW, 128), F32),
            pltpu.VMEM((2, LEVELS, 2, 128, 128), BF16),
            pltpu.VMEM((TLEV, cells, BPL * BS, NNZ_DEV * BS), BF16),
            pltpu.VMEM((cells, 2 * RW, NNZ_DEV * BS), BF16),
            pltpu.VMEM((cells, 2 * RW, NNZ_DEV * BS), BF16),
            pltpu.VMEM((TLEV, table_rows, 128), jnp.int32),
            pltpu.VMEM((TLEV, 8, 128), F32),
            pltpu.SMEM((TLEV, table_rows, 128), jnp.int32),
            pltpu.SMEM((TLEV, 8, 128), F32),
            pltpu.VMEM((128, RW, 128), F32),
            pltpu.VMEM((129, RW, 128), F32),
            pltpu.VMEM((TLEV - 1, units * 2, RW, 128), F32),
            pltpu.VMEM((TLEV, ny, nz, 2 * RW, 128), BF16),
            pltpu.VMEM((nz, 2, RW, 128), F32),
            pltpu.VMEM((TLEV, ny - 1, nz, 2 * RW, 128), BF16),
            pltpu.VMEM((TLEV, nz - 1, 2 * RW, 128), BF16),
            pltpu.VMEM((TLEV, nz - 1, 2 * RW, 128), BF16),
            pltpu.VMEM((LEVELS, 2, RW, 128), F32),
            pltpu.VMEM((TLEV, ny, nz, 2 * RW, 128), BF16),
            pltpu.VMEM((TLEV * cols, RW, 128), F32),
            pltpu.VMEM((LEVELS, 2, RW, 128), F32),
            pltpu.VMEM((LEVELS, cells, RW, 128), F32),
            pltpu.SemaphoreType.DMA((8,)),
            pltpu.SemaphoreType.DMA((2, TLEV)),
            pltpu.SemaphoreType.DMA((TLEV + 3,)),
            pltpu.SemaphoreType.DMA((2,)),
            pltpu.SemaphoreType.DMA((2 * TLEV * parts,)),
            pltpu.SemaphoreType.DMA((2 * TLEV * parts,)),
            pltpu.SemaphoreType.DMA((2 * TLEV * parts,)),
            pltpu.SemaphoreType.DMA((2 * TLEV * parts,)),
            pltpu.SemaphoreType.DMA,
            pltpu.SemaphoreType.DMA((LEVELS,)),
        ],
        compiler_params=pltpu.CompilerParams(
            collective_id=0, has_side_effects=True, vmem_limit_bytes=58 * 1024 * 1024
        ),
    )(pairs_of(right_side), pairs_of(diag_inverse), tile_rows, pan)
    result = result.reshape(LEVELS, -1, BPL, 128).transpose(0, 2, 1, 3)
    return result.reshape(LEVELS, BPL, -1)


def solution(mesh):
    in_specs = (
        P(None, "col", None),
        P(None, "col", None),
        P(None, "col", None, "row"),
        P(None, "col", "row"),
    )
    out_specs = P(None, "col", None)
    return jax.shard_map(local, mesh=mesh, in_specs=in_specs, out_specs=out_specs, check_vma=False)
```

```python
import functools

import jax
import jax.numpy as jnp
from jax import lax
from jax.experimental import pallas as pl
from jax.experimental.pallas import tpu as pltpu
from jax.sharding import PartitionSpec as P

BS = 64
LEVELS = 5
BPL = 2
NNZ_DEV = 8
TLEV = 4
RW = 8
MESH = pl.DeviceIdType.MESH
F32 = jnp.float32
BF16 = jnp.bfloat16
BOUNDS = (0, 3, 9, 16)
NT_DIMS = (((1,), (1,)), ((), ()))
NN_DIMS = (((1,), (0,)), ((), ()))


def sizes(owners):
    nz = 16 if owners % 32 == 0 else owners // 4
    return owners // 2 // nz, nz


def groups_of(nz):
    bounds = BOUNDS if nz == 16 else (0, max(1, nz // 2 - 1), nz)
    return tuple(zip(bounds[:-1], bounds[1:]))


def split(value):
    high = value.astype(BF16)
    return high, (value - high.astype(F32)).astype(BF16)


def product(value, pair, dims):
    rows = value.shape[0]
    high, rest = split(value)
    both = jnp.concatenate([high.astype(F32), rest.astype(F32)], axis=0).astype(BF16)
    first = lax.dot_general(both, pair[0], dims, preferred_element_type=F32)
    second = lax.dot_general(high, pair[1], dims, preferred_element_type=F32)
    return first[:rows] + (first[rows:] + second)


def kernel(
    owners,
    rows,
    rs_far,
    di_far,
    tr,
    pan,
    out,
    rs,
    di,
    trg,
    flip,
    bt,
    bu,
    ddc,
    pg,
    p0s,
    p0r,
    tbl,
    keepv,
    tbs,
    keeps,
    pd,
    cs,
    acc,
    sb,
    own,
    ry,
    sz,
    rz,
    ys,
    xu,
    xs,
    fx,
    osc,
    cell_sem,
    pan_sem,
    loc_sem,
    tab_sem,
    y_send,
    y_recv,
    z_send,
    z_recv,
    f_send,
    f_recv,
):
    ny, nz = sizes(owners)
    units = owners // 2
    cols = owners * BPL
    cells = 2 * rows
    per = BPL * NNZ_DEV
    tiles = cells * per
    chunks = (TLEV * cols + 127) // 128
    groups = groups_of(nz)
    parts = len(groups)
    col = lax.axis_index("col")
    x = lax.axis_index("row")
    c = col & 1
    z = (col // 2) & (nz - 1)
    y = col // (2 * nz)
    me = x * 2 + c

    def at(x_to, y_to, z_to, c_to):
        return {"row": x_to, "col": (y_to * nz + z_to) * 2 + c_to}

    def cell_peer(j):
        other = (me + j) & (cells - 1)
        return other, at(other // 2, y, z, other & 1)

    def y_peer(j):
        return at(x, (y + j) & (ny - 1), z, c)

    def step(p):
        half = (p + 1) // 2
        return nz // 2 + (half if p % 2 == 0 else -half)

    def facing(p):
        return p if step(p) in (0, nz // 2) else p + 1 if p % 2 == 1 else p - 1

    def z_peer(p):
        return at(x, y, (z + step(p)) & (nz - 1), c)

    def unit_of(j, p):
        return ((y + j) & (ny - 1)) * nz + ((z + step(p)) & (nz - 1))

    def send(src, dst, send_sem, recv_sem, device):
        pltpu.make_async_remote_copy(
            src_ref=src,
            dst_ref=dst,
            send_sem=send_sem,
            recv_sem=recv_sem,
            device_id=device,
            device_id_type=MESH,
        ).start()

    def settle(ref, sem):
        pltpu.make_async_copy(ref, ref, sem).wait()

    def low_of(count):
        return lax.broadcasted_iota(jnp.int32, (count, 128), 1) < BS

    low = low_of(RW)
    low32 = low_of(32)

    pltpu.make_async_copy(rs_far, rs, loc_sem.at[TLEV]).start()
    pltpu.make_async_copy(di_far, di, loc_sem.at[TLEV + 1]).start()
    pltpu.make_async_copy(tr, trg.at[me], loc_sem.at[TLEV + 2]).start()
    for t in range(TLEV):
        pltpu.make_async_copy(pan.at[t], pg.at[t, me], loc_sem.at[t]).start()

    barrier = pltpu.get_barrier_semaphore()

    def greet(device):
        pl.semaphore_signal(barrier, inc=1, device_id=device, device_id_type=MESH)

    for p in range(nz - 1):
        greet(z_peer(p))
    for j in range(1, ny):
        greet(y_peer(j))
    for j in range(1, cells):
        greet(cell_peer(j)[1])

    pltpu.make_async_copy(rs_far, rs, loc_sem.at[TLEV]).wait()
    pltpu.make_async_copy(di_far, di, loc_sem.at[TLEV + 1]).wait()
    pltpu.make_async_copy(tr, trg.at[me], loc_sem.at[TLEV + 2]).wait()
    for t in range(LEVELS):
        for k in range(BPL):
            value = rs[t, pl.ds(k, 32, 2), :]
            flip[t, pl.ds(k * BS, 32, 2), :] = value
            flip[t, pl.ds(k * BS + 1, 32, 2), :] = pltpu.roll(value, BS, 1)
            value = di[t, pl.ds(k, 32, 2), :]
            turned = pltpu.roll(value, BS, 1)
            keep = low32 if k == 0 else jnp.logical_not(low32)
            for par in range(2):
                half = value if par == k else turned
                flip[LEVELS + t, pl.ds(k * BS + par, 32, 2), :] = jnp.where(keep, half, 0.0)
    cells_r = cells * RW
    for t in range(LEVELS):
        turned = flip[t].T
        for q in range(cells):
            bt[t, q] = turned[q * RW : (q + 1) * RW]
        high, rest = split(flip[LEVELS + t])
        ddc[c, t, 0] = high
        ddc[c, t, 1] = rest
    for t in range(LEVELS):
        bu[c, t] = bt[t, me]

    right = bt[0].reshape(cells_r, 128)
    solved = product(right, (ddc[c, 0, 0], ddc[c, 0, 1]), NT_DIMS)
    pieces = []
    for q in range(cells):
        value = solved[q * RW : (q + 1) * RW]
        pieces += [jnp.where(low, value, 0.0), jnp.where(low, 0.0, value)]
    pltpu.make_async_copy(pan.at[0], pg.at[0, me], loc_sem.at[0]).wait()
    value = lax.dot_general(
        jnp.concatenate(pieces, axis=0).astype(BF16),
        pg[0, me],
        NN_DIMS,
        preferred_element_type=F32,
    ).astype(BF16)
    for q in range(cells):
        p0s[q] = value[q * 2 * RW : (q + 1) * 2 * RW]

    pl.semaphore_wait(barrier, cells - 1 + ny - 1 + nz - 1)

    for j in range(1, cells):
        other, device = cell_peer(j)
        send(tr, trg.at[me], cell_sem.at[0], cell_sem.at[1], device)
    for j in range(1, cells):
        other, device = cell_peer(j)
        send(p0s.at[other], p0r.at[me], cell_sem.at[6], cell_sem.at[7], device)
    core_peer = at(x, y, z, 1 - c)
    send(bt.at[:, me + 1 - 2 * c], bu.at[c], cell_sem.at[2], cell_sem.at[3], core_peer)
    send(ddc.at[c], ddc.at[c], cell_sem.at[4], cell_sem.at[5], core_peer)

    def send_panels(t):
        for j in range(1, cells):
            device = cell_peer(j)[1]
            send(pan.at[t], pg.at[t, me], pan_sem.at[0, t], pan_sem.at[1, t], device)

    send_panels(1)
    p0r[me] = p0s[me]

    settle(trg.at[pl.ds(0, cells - 1)], cell_sem.at[1])
    pieces = [trg[q, :, k, :] for q in range(cells) for k in range(BPL)]
    if tiles < 128:
        pieces.append(jnp.full((TLEV, 128 - tiles), 1 << 20, jnp.int32))
    targets = jnp.concatenate(pieces, axis=1)
    square = (128, 128)
    above = lax.broadcasted_iota(jnp.int32, square, 0)
    lane = lax.broadcasted_iota(jnp.int32, square, 1)
    def table(t):
        mine = jnp.broadcast_to(targets[t : t + 1, :], square)
        other = mine.T
        before = (other < mine) | ((other == mine) & (above < lane))
        rank = jnp.sum(before.astype(jnp.int32), axis=0, keepdims=True)
        placed = jnp.broadcast_to(rank, square).T == lane
        order = jnp.sum(jnp.where(placed, above, 0), axis=0, keepdims=True)
        ordered = jnp.sum(jnp.where(placed, other, 0), axis=0, keepdims=True)
        ordered8 = jnp.broadcast_to(ordered, (8, 128))
        first = lax.broadcasted_iota(jnp.int32, (8, 128), 1) == 0
        same = (ordered8 == pltpu.roll(ordered8, 1, 1)) & jnp.logical_not(first)
        keepv[t, 0:1, :] = same.astype(F32)[0:1]
        tbl[t, 0:1, :] = order
        source = jnp.clip(mine[0:1] - cols, 0, TLEV * cols - 1)
        tbl[t, 1:2, :] = source
        for chunk in range(t * cols // 128, chunks):
            slot = lane + (cols + chunk * 128)
            upto = jnp.sum((other <= slot).astype(jnp.int32), axis=0, keepdims=True)
            equal = jnp.sum((other == slot).astype(jnp.int32), axis=0, keepdims=True)
            tbl[t, 2 + chunk : 3 + chunk, :] = jnp.where(equal > 0, upto - 1, 128)
        pltpu.make_async_copy(tbl.at[t], tbs.at[t], tab_sem.at[0]).start()
        pltpu.make_async_copy(keepv.at[t], keeps.at[t], tab_sem.at[1]).start()

    def table_done(t):
        pltpu.make_async_copy(tbl.at[t], tbs.at[t], tab_sem.at[0]).wait()
        pltpu.make_async_copy(keepv.at[t], keeps.at[t], tab_sem.at[1]).wait()

    table(0)
    cs[128] = jnp.zeros((RW, 128), F32)

    def halves_of(t, level, u):
        number = (level - 1) * cols + u * 4
        row = 2 + lax.shift_right_logical(number, 7)
        place = number & 127
        found = [cs[tbs[t, row, place + k]] for k in range(4)]
        halves = [jnp.where(low, found[0], found[1]), jnp.where(low, found[2], found[3])]
        if t > 0:
            halves = [halves[h] + acc[level - 2, u * 2 + h] for h in range(2)]
        return halves

    def tile_pair(tile, value):
        turned = pltpu.roll(value, BS, 1)
        pd[tile] = jnp.where(low, value, turned)
        pd[tile + 1] = jnp.where(low, turned, value)

    def solve(t, core, remain, dims):
        return product(remain, (ddc[core, t, 0], ddc[core, t, 1]), dims)

    def forward(t, update):
        solved = []
        for core in range(2):
            remain = bu[core, t]
            if update is not None:
                remain = remain - update[core]
            value = solve(t, core, remain, NT_DIMS)
            ys[t, core] = value
            solved.append(value)
        return solved

    update = None
    for t in range(TLEV):
        if t == 0:
            settle(p0r.at[pl.ds(0, cells - 1)], cell_sem.at[7])
            for q in range(cells):
                value = p0r[q].astype(F32)
                for k in range(2):
                    for p in range(4):
                        part = value[k * RW : (k + 1) * RW, p * 128 : (p + 1) * 128]
                        tile_pair(q * per + k * NNZ_DEV + p * 2, part)
        else:
            solved = forward(t, update)
            nothing = jnp.zeros((RW, 128), F32)
            pieces = []
            for core in range(2):
                for k in range(2):
                    kept = jnp.where(low, solved[core], 0.0)
                    if k == 1:
                        kept = jnp.where(low, 0.0, solved[core])
                    side = [kept, nothing] if core == 0 else [nothing, kept]
                    pieces.append(jnp.concatenate(side, axis=1))
            vectors = jnp.concatenate(pieces, axis=0).astype(BF16)
            settle(pg.at[t, 0], loc_sem.at[t])
            settle(pg.at[t, pl.ds(0, cells - 1)], pan_sem.at[1, t])
            for group in range(rows):
                panel = pg[t, pl.ds(2 * group, 2)].reshape(4 * BS, NNZ_DEV * BS)
                value = lax.dot_general(vectors, panel, NN_DIMS, preferred_element_type=F32)
                for b in range(4):
                    for p in range(4):
                        part = value[b * RW : (b + 1) * RW, p * 128 : (p + 1) * 128]
                        tile_pair(group * 32 + b * 8 + p * 2, part)

        table_done(t)

        def scan(i, total, t=t):
            for k in range(32):
                place = i * 32 + k
                total = total * keeps[t, 0, place] + pd[tbs[t, 0, place]]
                cs[place] = total
            return total

        lax.fori_loop(0, tiles // 32, scan, jnp.zeros((RW, 128), F32))

        for g, (begin, end) in enumerate(groups):

            @pl.loop(0, ny - 1)
            def _(i, t=t, g=g, begin=begin, end=end):
                j = jnp.where(i == 0, ny // 2, jnp.where(i < ny // 2 + (ny == 2), i, i + 1))
                for p in range(begin, end):
                    halves = halves_of(t, t + 1, unit_of(j, p))
                    sb[t, j, p] = jnp.concatenate(halves, axis=0).astype(BF16)
                there = pl.ds(begin, end - begin)
                send(
                    sb.at[t, j, there],
                    ry.at[t, j - 1, there],
                    y_send.at[parts * t + g],
                    y_recv.at[parts * t + g],
                    y_peer(j),
                )

        for p in range(nz):
            halves = halves_of(t, t + 1, unit_of(0, p))
            own[p, 0] = halves[0]
            own[p, 1] = halves[1]
        def partial(p, t=t):
            halves = []
            for h in range(2):
                value = own[p, h]
                for j in range(ny - 1):
                    value = value + ry[t, j, p].astype(F32)[h * RW : (h + 1) * RW]
                halves.append(value)
            return halves

        for g, (begin, end) in enumerate(groups):
            settle(ry.at[t, :, pl.ds(begin, end - begin)], y_recv.at[parts * t + g])
            for p in range(begin, min(end, nz - 1)):
                sz[t, p] = jnp.concatenate(partial(p), axis=0).astype(BF16)
                send(
                    sz.at[t, p],
                    rz.at[t, p],
                    z_send.at[parts * t],
                    z_recv.at[parts * t + g],
                    z_peer(p),
                )
        if t + 2 < TLEV:
            send_panels(t + 2)
        for level in range(t + 2, LEVELS):

            @pl.loop(0, units // 4)
            def _(i, t=t, level=level):
                for k in range(4):
                    u = i * 4 + k
                    halves = halves_of(t, level, u)
                    acc[level - 2, u * 2] = halves[0]
                    acc[level - 2, u * 2 + 1] = halves[1]

        if t == 0:
            settle(bu.at[0], cell_sem.at[3])
            settle(ddc.at[0], cell_sem.at[5])
            forward(0, None)
        if t + 1 < TLEV:
            table(t + 1)

        update = partial(nz - 1)
        for g, (begin, end) in reversed(list(enumerate(groups))):
            count = min(end, nz - 1) - begin
            if count > 0:
                settle(rz.at[t, pl.ds(begin, count)], z_recv.at[parts * t + g])
            for p in range(begin, begin + count):
                arrived = rz[t, p].astype(F32)
                update = [update[0] + arrived[:RW], update[1] + arrived[RW:]]

    send_panels(0)
    forward(TLEV, update)

    def finish(t):
        settle(osc.at[t, pl.ds(0, cells - 1)], f_recv.at[t])
        value = osc[t].reshape(cells_r, 128)
        if cells_r < 128:
            value = jnp.concatenate([value] * (128 // cells_r), axis=0)
        flip[t] = value.T
        for k in range(BPL):
            even = flip[t, pl.ds(k * BS, 32, 2), :]
            odd = flip[t, pl.ds(k * BS + 1, 32, 2), :]
            out[t, pl.ds(k, 32, 2), :] = jnp.where(low32, even, odd)

    for t in range(LEVELS - 1, -1, -1):
        if t < TLEV:
            if t == 0:
                settle(pg.at[0, pl.ds(0, cells - 1)], pan_sem.at[1, 0])
            weighted = None
            for group in range(rows):
                lines = []
                for b in range(4):
                    line = []
                    for p in range(4):
                        tile = group * 32 + b * 8 + p * 2
                        first = xs[tbs[t, 1, tile]]
                        second = xs[tbs[t, 1, tile + 1]]
                        line.append(jnp.where(low, first, second))
                    lines.append(jnp.concatenate(line, axis=1))
                picked = jnp.concatenate(lines, axis=0).astype(BF16)
                panel = pg[t, pl.ds(2 * group, 2)].reshape(4 * BS, NNZ_DEV * BS)
                value = lax.dot_general(picked, panel, NT_DIMS, preferred_element_type=F32)
                weighted = value if weighted is None else weighted + value
        results = []
        for core in range(2):
            remain = ys[t, core]
            if t < TLEV:
                lanes = slice(core * 128, core * 128 + 128)
                remain = remain - jnp.where(
                    low,
                    weighted[core * 16 : core * 16 + 8, lanes],
                    weighted[core * 16 + 8 : core * 16 + 16, lanes],
                )
            value = solve(t, core, remain, NN_DIMS)
            fx[t, core] = value
            results.append(value)
        n = TLEV + t - 1
        if t > 0:
            xu[t - 1, 0, nz - 1] = jnp.concatenate(results, axis=0).astype(BF16)
            for p in range(nz - 1):
                seen = facing(p)
                g = [begin <= seen < end for begin, end in groups].index(True)
                send(
                    xu.at[t - 1, 0, nz - 1],
                    xu.at[t - 1, 0, seen],
                    z_send.at[parts * n],
                    z_recv.at[parts * n + g],
                    z_peer(p),
                )

        osc[t, me] = fx[t, c]
        for j in range(1, cells):
            other, device = cell_peer(j)
            send(fx.at[t, other & 1], osc.at[t, me], f_send, f_recv.at[t], device)
        if t + 1 < LEVELS:
            finish(t + 1)

        if t > 0:

            def expand(j, p, t=t):
                value = xu[t - 1, j, p].astype(F32)
                slot = (t - 1) * cols + unit_of(j, p) * 4
                for h in range(2):
                    half = value[h * RW : (h + 1) * RW]
                    turned = pltpu.roll(half, BS, 1)
                    xs[slot + 2 * h] = jnp.where(low, half, turned)
                    xs[slot + 2 * h + 1] = jnp.where(low, turned, half)

            for g, (begin, end) in reversed(list(enumerate(groups))):
                count = min(end, nz - 1) - begin
                if count > 0:
                    settle(xu.at[t - 1, 0, pl.ds(begin, count)], z_recv.at[parts * n + g])
                there = pl.ds(begin, end - begin)
                for j in range(1, ny):
                    send(
                        xu.at[t - 1, 0, there],
                        xu.at[t - 1, ny - j, there],
                        y_send.at[parts * n + g],
                        y_recv.at[parts * n + g],
                        y_peer(j),
                    )
                for p in range(begin, end):
                    expand(0, p)
            for g, (begin, end) in reversed(list(enumerate(groups))):
                there = pl.ds(begin, end - begin)
                settle(xu.at[t - 1, pl.ds(1, ny - 1), there], y_recv.at[parts * n + g])

                @pl.loop(1, ny)
                def _(j, begin=begin, end=end):
                    for p in range(begin, end):
                        expand(j, p)

    finish(0)

    settle(trg.at[pl.ds(0, cells - 1)], cell_sem.at[0])
    settle(bu.at[0], cell_sem.at[2])
    settle(ddc.at[0], cell_sem.at[4])
    settle(p0r.at[pl.ds(0, cells - 1)], cell_sem.at[6])
    for t in range(TLEV):
        settle(pg.at[t, pl.ds(0, cells - 1)], pan_sem.at[0, t])
        settle(rz.at[t], z_send.at[parts * t])
        settle(xu.at[t, 0, pl.ds(0, nz - 1)], z_send.at[parts * (TLEV + t)])
        for g, (begin, end) in enumerate(groups):
            there = pl.ds(begin, end - begin)
            settle(ry.at[t, :, there], y_send.at[parts * t + g])
            settle(xu.at[t, pl.ds(1, ny - 1), there], y_send.at[parts * (TLEV + t) + g])
    for t in range(LEVELS):
        settle(osc.at[t, pl.ds(0, cells - 1)], f_send)


def pairs_of(value):
    value = value.reshape(LEVELS, BPL, -1, 128).transpose(0, 2, 1, 3)
    return value.reshape(LEVELS, -1, 128)


def local(right_side, diag_inverse, panels, tile_rows):
    owners = lax.axis_size("col")
    rows = lax.axis_size("row")
    ny, nz = sizes(owners)
    parts = len(groups_of(nz))
    units = owners // 2
    cols = owners * BPL
    cells = 2 * rows
    chunks = (TLEV * cols + 127) // 128
    table_rows = (2 + chunks + 7) // 8 * 8
    pan = panels.reshape(TLEV, BPL * BS, NNZ_DEV * BS)
    vmem = pl.BlockSpec(memory_space=pltpu.VMEM)
    far = pl.BlockSpec(memory_space=pltpu.HBM)
    result = pl.pallas_call(
        functools.partial(kernel, owners, rows),
        out_shape=jax.ShapeDtypeStruct((LEVELS, BS, 128), F32),
        in_specs=[far, far, far, far],
        out_specs=vmem,
        scratch_shapes=[
            pltpu.VMEM((LEVELS, BS, 128), F32),
            pltpu.VMEM((LEVELS, BS, 128), F32),
            pltpu.VMEM((cells, TLEV, BPL, NNZ_DEV), jnp.int32),
            pltpu.VMEM((2 * LEVELS, 128, 128), F32),
            pltpu.VMEM((LEVELS, cells, RW, 128), F32),
            pltpu.VMEM((2, LEVELS, RW, 128), F32),
            pltpu.VMEM((2, LEVELS, 2, 128, 128), BF16),
            pltpu.VMEM((TLEV, cells, BPL * BS, NNZ_DEV * BS), BF16),
            pltpu.VMEM((cells, 2 * RW, NNZ_DEV * BS), BF16),
            pltpu.VMEM((cells, 2 * RW, NNZ_DEV * BS), BF16),
            pltpu.VMEM((TLEV, table_rows, 128), jnp.int32),
            pltpu.VMEM((TLEV, 8, 128), F32),
            pltpu.SMEM((TLEV, table_rows, 128), jnp.int32),
            pltpu.SMEM((TLEV, 8, 128), F32),
            pltpu.VMEM((128, RW, 128), F32),
            pltpu.VMEM((129, RW, 128), F32),
            pltpu.VMEM((TLEV - 1, units * 2, RW, 128), F32),
            pltpu.VMEM((TLEV, ny, nz, 2 * RW, 128), BF16),
            pltpu.VMEM((nz, 2, RW, 128), F32),
            pltpu.VMEM((TLEV, ny - 1, nz, 2 * RW, 128), BF16),
            pltpu.VMEM((TLEV, nz - 1, 2 * RW, 128), BF16),
            pltpu.VMEM((TLEV, nz - 1, 2 * RW, 128), BF16),
            pltpu.VMEM((LEVELS, 2, RW, 128), F32),
            pltpu.VMEM((TLEV, ny, nz, 2 * RW, 128), BF16),
            pltpu.VMEM((TLEV * cols, RW, 128), F32),
            pltpu.VMEM((LEVELS, 2, RW, 128), F32),
            pltpu.VMEM((LEVELS, cells, RW, 128), F32),
            pltpu.SemaphoreType.DMA((8,)),
            pltpu.SemaphoreType.DMA((2, TLEV)),
            pltpu.SemaphoreType.DMA((TLEV + 3,)),
            pltpu.SemaphoreType.DMA((2,)),
            pltpu.SemaphoreType.DMA((2 * TLEV * parts,)),
            pltpu.SemaphoreType.DMA((2 * TLEV * parts,)),
            pltpu.SemaphoreType.DMA((2 * TLEV * parts,)),
            pltpu.SemaphoreType.DMA((2 * TLEV * parts,)),
            pltpu.SemaphoreType.DMA,
            pltpu.SemaphoreType.DMA((LEVELS,)),
        ],
        compiler_params=pltpu.CompilerParams(
            collective_id=0, has_side_effects=True, vmem_limit_bytes=58 * 1024 * 1024
        ),
    )(pairs_of(right_side), pairs_of(diag_inverse), tile_rows, pan)
    result = result.reshape(LEVELS, -1, BPL, 128).transpose(0, 2, 1, 3)
    return result.reshape(LEVELS, BPL, -1)


def solution(mesh):
    in_specs = (
        P(None, "col", None),
        P(None, "col", None),
        P(None, "col", None, "row"),
        P(None, "col", "row"),
    )
    out_specs = P(None, "col", None)
    return jax.shard_map(local, mesh=mesh, in_specs=in_specs, out_specs=out_specs, check_vma=False)
```
